256 devices in a mesh: grp: 4 (over z_lo, core), dev: 64 (over y, z_hi, x).
Axes of the slice: x: 4, y: 4, z: 8 (z_hi: 4, z_lo: 2; z = z_hi * 2 + z_lo), core: 2. Of those that a mesh axis runs over, the one named last changes fastest.
Arguments:
- gradient: bfloat16 [64, 512, 2048], P('grp', 'dev'), may hold values from -400 to 400
- momentum: float32 [256, 512, 512], P(('grp', 'dev')), may hold values from -8 to 8
- master_weight: float32 [256, 512, 512], P(('grp', 'dev')), may hold values from -0.12 to 0.12
- owned_matrix: int32 [4, 16], replicated, may hold values from 0 to 15, each once within a row
- rollout_matrix: int32 [4, 64], P('grp'), may hold values from 0 to 63, each once within a row
Outputs:
- new_momentum: float32 [256, 512, 512], P(('grp', 'dev'))
- update: float32 [256, 512, 512], P(('grp', 'dev'))
- new_master: float32 [256, 512, 512], P(('grp', 'dev'))
- rollout_weight: bfloat16 [256, 512, 2048], P(('grp', 'dev'))
The draws below stay inside these ranges and needn't reach their ends.
Inputs may be any that keep to these rules, and one draw needn't show every extreme that they name: Each row of owned_matrix lists every number 0 to 15 once. Each row of rollout_matrix lists every matrix 0 to 63 once.
All inputs are finite; a program needn't handle non-finite values.
Results may differ from the reference program's by a relative error of at most 0.001.
Values may be sent and summed in bfloat16 or wider, within the bound.
A program may use at most 64 MiB of HBM per device.

```python
import math
import jax
import jax.numpy as jnp
from jax import lax

ROWS = 512
COLS = 2048
SPLIT = 4
ITERS = 5
SLAB = 512
QUADS = 16
MATS = 64
OWNED = 256
N_GRP = 4


def draw_gradient(key, part):
    first_key, second_key, third_key = jax.random.split(jax.random.fold_in(key, 71), 3)
    base = jnp.clip(jax.random.normal(first_key, (MATS, ROWS, COLS), jnp.float32), -4.0, 4.0)
    top_log = jnp.log(10.0)
    row_scale = jnp.exp(jax.random.uniform(second_key, (MATS, ROWS, 1), jnp.float32, 0.0, 1.0) * top_log)
    col_scale = jnp.exp(jax.random.uniform(third_key, (MATS, 1, COLS), jnp.float32, 0.0, 1.0) * top_log)
    scaled = base * row_scale * col_scale * (100.0 / 256.0)
    return scaled.astype(jnp.bfloat16)


def block_scale(own_key, shape, pieces, smallest, top_value):
    loudness, own = 1.0, jax.random.fold_in(own_key, 6)
    for dim, parts in pieces:
        steps = jnp.exp(jax.random.uniform(jax.random.fold_in(own, dim), (parts,), jnp.float32, smallest / len(pieces), top_value / len(pieces)))
        loudness = loudness * jnp.repeat(steps, shape[dim] // parts).reshape([-1 if axis == dim else 1 for axis in range(len(shape))])
    return loudness


def gaussian(rng, extent, deviation, limit, cuts=(), kind=jnp.bfloat16):
    values = jax.random.normal(rng, extent, jnp.float32) * deviation
    if len(cuts) > 0:
        values = block_scale(rng, extent, cuts, -0.22, 0.18) * values
    return jnp.clip(values, min=-limit, max=limit).astype(kind)


def setup_inputs(seed: int = 0) -> dict:
    key_list = jax.random.split(jax.random.key(seed), 6)
    gradient = draw_gradient(jax.random.fold_in(key_list[5], 71), 0)
    momentum = gaussian(key_list[1], (OWNED, ROWS, SLAB), 3.0, 8.0, ((0, 256),), jnp.float32)
    master_weight = gaussian(key_list[2], (OWNED, ROWS, SLAB), 0.02, 0.12, ((0, 256),), jnp.float32)
    owned_matrix = jax.vmap(lambda own: jax.random.permutation(own, QUADS))(jax.random.split(key_list[3], N_GRP)).reshape((N_GRP, QUADS)).astype(jnp.int32)
    rollout_matrix = jax.vmap(lambda own: jax.random.permutation(own, MATS))(jax.random.split(key_list[4], N_GRP)).reshape((N_GRP, MATS)).astype(jnp.int32)
    return dict(gradient=gradient, momentum=momentum, master_weight=master_weight, owned_matrix=owned_matrix, rollout_matrix=rollout_matrix)


momentum_decay = 0.95
learn_rate = 0.02
weight_decay = 0.1
first_coeff = 3.4445
second_coeff = -4.775
third_coeff = 2.0315
norm_epsilon = 1e-07

def product(left, right):
    return jnp.dot(left, right, precision=lax.Precision.HIGHEST, preferred_element_type=jnp.float32)

def orthogonal(matrix):
    current = matrix * (1.0 / (jnp.sqrt(jnp.sum(matrix * matrix)) + norm_epsilon))
    for step_index in range(ITERS):
        square = product(current, current.T)
        mixed = second_coeff * square + third_coeff * product(square, square)
        current = first_coeff * current + product(mixed, current)
    return current

def reference(gradient, momentum, master_weight, owned_matrix, rollout_matrix):
    groups = owned_matrix.shape[0]
    quads = owned_matrix.shape[1]
    owners = groups * quads
    slab_cols = COLS // SPLIT

    def assemble(slabs):
        return slabs.reshape(owners, SPLIT, ROWS, slab_cols).transpose(0, 2, 1, 3).reshape(owners, ROWS, COLS)

    def split_back(full):
        return full.reshape(owners, ROWS, SPLIT, slab_cols).transpose(0, 2, 1, 3).reshape(owners * SPLIT, ROWS, slab_cols)
    global_id = (jnp.arange(groups, dtype=jnp.int32)[:, None] * quads + owned_matrix.astype(jnp.int32)).reshape(-1)
    chosen = gradient[global_id].astype(jnp.float32)
    moment = assemble(momentum)
    master = assemble(master_weight)
    new_moment = momentum_decay * moment + chosen
    nesterov = chosen + momentum_decay * new_moment
    scale_factor = 0.2 * math.sqrt(max(ROWS, COLS))
    update = lax.map(orthogonal, nesterov) * scale_factor
    new_weight = master - learn_rate * (update + weight_decay * master)
    rounded = new_weight.astype(jnp.bfloat16)
    position = jnp.zeros((owners,), jnp.int32).at[global_id].set(jnp.arange(owners, dtype=jnp.int32))
    rollout = rounded[position[rollout_matrix.reshape(-1).astype(jnp.int32)]]
    return (split_back(new_moment), split_back(update), split_back(new_weight), rollout)
```

```python
import math

import jax
import jax.numpy as jnp
from jax import lax
from jax.experimental import pallas as pl
from jax.experimental.pallas import tpu as pltpu
from jax.sharding import PartitionSpec as P

MESH = pl.DeviceIdType.MESH
F32 = jnp.float32
BF16 = jnp.bfloat16

ITERS = 5
momentum_decay = 0.95
learn_rate = 0.02
weight_decay = 0.1
first_coeff = 3.4445
second_coeff = -4.775
third_coeff = 2.0315
norm_epsilon = 1e-07

N = 512
HALF = 256
QUADS = 16
DEVS = 64
CHUNKS = 4
DEPTH = 64 // CHUNKS
TILES = [(i, j) for i in range(4) for j in range(i, 4)]
PIECE = len(TILES) * 128 // 4


def place():
    grp, dev = lax.axis_index("grp"), lax.axis_index("dev")
    return dev % 4, dev // 16, (dev // 4) % 4, grp // 2, grp % 2


def split2(value):
    high = value.astype(BF16)
    return high, (value - high.astype(F32)).astype(BF16)


def split3(value):
    high = value.astype(BF16)
    rest = value - high.astype(F32)
    mid = rest.astype(BF16)
    return high, mid, (rest - mid.astype(F32)).astype(BF16)


def dot(left, right):
    return jnp.dot(left, right, preferred_element_type=F32)


def dot_t(left, right):
    return lax.dot_general(left, right, (((1,), (1,)), ((), ())), preferred_element_type=F32)


def terms(count):
    pairs = [(i, j) for i in range(count) for j in range(count) if i + j < count]
    return sorted(pairs, key=lambda pair: -sum(pair))


def gram_kernel(
    owned, grad, mom, slab_out, gram_out,
    outbox, inbox, parts, partial, others, full,
    send_sem, recv_sem, rs_send, rs_recv, ag_send, ag_recv,
):
    grp, dev = lax.axis_index("grp"), lax.axis_index("dev")
    x = dev % 4
    barrier = pltpu.get_barrier_semaphore()

    def greet(step, carry):
        pl.semaphore_signal(barrier, inc=1, device_id=(grp, (dev + step) % DEVS), device_id_type=MESH)
        return carry

    lax.fori_loop(1, DEVS, greet, 0)

    def fill(q, carry):
        rows = grad[owned[grp, q]].astype(F32)
        for c in range(4):
            left = rows[:, c * N : c * N + HALF]
            right = rows[:, c * N + HALF : (c + 1) * N]
            outbox[q * 4 + c] = jnp.concatenate([left, right], axis=0).astype(BF16)
        return carry

    lax.fori_loop(0, QUADS, fill, 0)
    pl.semaphore_wait(barrier, DEVS - 1)

    def send(step, carry):
        to = (dev + step) % DEVS
        pltpu.make_async_remote_copy(
            src_ref=outbox.at[to], dst_ref=inbox.at[dev], send_sem=send_sem, recv_sem=recv_sem,
            device_id=(grp, to), device_id_type=MESH,
        ).start()
        return carry

    lax.fori_loop(1, DEVS, send, 0)
    inbox[dev] = outbox[dev]
    rest = pl.ds(0, DEVS - 1)
    everything = pltpu.make_async_remote_copy(
        src_ref=outbox.at[rest], dst_ref=inbox.at[rest], send_sem=send_sem, recv_sem=recv_sem,
        device_id=(grp, (dev + 1) % DEVS), device_id_type=MESH,
    )
    everything.wait_recv()

    for r in range(4):
        got = inbox[pl.ds(r * 16, 16)].astype(F32)
        slab = jnp.concatenate(
            [got[:, :8, :].reshape(128, HALF), got[:, 8:, :].reshape(128, HALF)], axis=1
        )
        rows = pl.ds(r * 128, 128)
        slab_out[rows, :] = slab.astype(BF16)
        moment = momentum_decay * mom[rows, :] + slab
        for index, part in enumerate(split3(slab + momentum_decay * moment)):
            parts[index, rows, :] = part

    at = 0
    for i in range(4):
        total = None
        for a, b in terms(3):
            term = dot_t(parts[a, i * 128 : (i + 1) * 128, :], parts[b, i * 128 :, :])
            total = term if total is None else total + term
        for j in range(4 - i):
            for h in range(2):
                unit = 2 * at + h
                partial[unit // 5, (unit % 5) * 64 : (unit % 5 + 1) * 64, :] = total[
                    h * 64 : (h + 1) * 64, j * 128 : (j + 1) * 128
                ]
            at += 1

    def share(step, src, dst, sends, recvs):
        return pltpu.make_async_remote_copy(
            src_ref=src, dst_ref=dst, send_sem=sends.at[step - 1], recv_sem=recvs.at[step - 1],
            device_id=(grp, dev - x + (x + step) % 4), device_id_type=MESH,
        )

    scatter = [
        share(step, partial.at[(x + step) % 4], others.at[step - 1], rs_send, rs_recv)
        for step in (2, 1, 3)
    ]
    for copy in scatter:
        copy.start()
    for copy in scatter:
        copy.wait_recv()
    full[x] = (partial[x] + others[0]) + (others[1] + others[2])
    gather = [share(step, full.at[x], full.at[x], ag_send, ag_recv) for step in (2, 1, 3)]
    for copy in gather:
        copy.start()
    everything.wait_send()
    for copy in scatter:
        copy.wait_send()
    for copy in gather:
        copy.wait()
    for index in range(4):
        gram_out[index * PIECE : (index + 1) * PIECE, :] = full[index]


def gram_call(owned, grad, mom):
    vmem = pl.BlockSpec(memory_space=pltpu.VMEM)
    dma = pltpu.SemaphoreType.DMA
    return pl.pallas_call(
        gram_kernel,
        out_shape=(
            jax.ShapeDtypeStruct((N, N), BF16),
            jax.ShapeDtypeStruct((4 * PIECE, 128), F32),
        ),
        in_specs=[pl.BlockSpec(memory_space=pltpu.SMEM), vmem, vmem],
        out_specs=(vmem, vmem),
        scratch_shapes=[
            pltpu.VMEM((DEVS, 16, HALF), BF16),
            pltpu.VMEM((DEVS, 16, HALF), BF16),
            pltpu.VMEM((3, N, N), BF16),
            pltpu.VMEM((4, PIECE, 128), F32),
            pltpu.VMEM((3, PIECE, 128), F32),
            pltpu.VMEM((4, PIECE, 128), F32),
            dma, dma, dma((3,)), dma((3,)), dma((3,)), dma((3,)),
        ],
        compiler_params=pltpu.CompilerParams(
            collective_id=0, has_side_effects=True, vmem_limit_bytes=40 << 20
        ),
        name="gram",
    )(owned, grad, mom)


def ns_kernel(
    mom, slab, master, gram, mom_out, update_out, master_out, rounded_out,
    a_ref, b_ref, t_ref, x_ref, p0, p1, p2, q0, q1, q2,
):
    scale = None
    for at, (i, j) in enumerate(TILES):
        block = gram[at * 128 : (at + 1) * 128, :]
        a_ref[i * 128 : (i + 1) * 128, j * 128 : (j + 1) * 128] = block
        if i != j:
            a_ref[j * 128 : (j + 1) * 128, i * 128 : (i + 1) * 128] = block.T
        else:
            row = lax.broadcasted_iota(jnp.int32, (128, 128), 0)
            col = lax.broadcasted_iota(jnp.int32, (128, 128), 1)
            trace = jnp.sum(jnp.where(row == col, block, 0.0))
            scale = trace if scale is None else scale + trace
    factor = 1.0 / (jnp.sqrt(jnp.full((1, 1), scale, F32)) + norm_epsilon)

    lefts, rights = (p0, p1, p2), (q0, q1, q2)

    def load(slots, value_ref, count):
        for r in range(4):
            rows = slice(r * 128, (r + 1) * 128)
            value = value_ref[rows, :]
            for slot, part in zip(slots, split2(value) if count == 2 else split3(value)):
                slot[rows, :] = part

    def block(rows, cols, count):
        total = None
        for a, b in terms(count):
            term = dot(lefts[a][rows, :], rights[b][:, cols])
            total = term if total is None else total + term
        return total

    low, high = slice(0, HALF), slice(HALF, N)

    def symmetric(dst, count, finish):
        for r in range(2):
            rows = slice(r * 128, (r + 1) * 128)
            top = block(rows, slice(0, N), count)
            dst[rows, :] = finish(top, rows, slice(0, N))
        for r in range(2, 4):
            rows = slice(r * 128, (r + 1) * 128)
            dst[rows, HALF:] = finish(block(rows, high, count), rows, high)
        for r in range(2):
            for s in range(2, 4):
                dst[s * 128 : (s + 1) * 128, r * 128 : (r + 1) * 128] = dst[
                    r * 128 : (r + 1) * 128, s * 128 : (s + 1) * 128
                ].T

    def iterate(count, last):
        load(lefts, a_ref, count)
        load(rights, a_ref, count)
        symmetric(
            b_ref, count,
            lambda v, r, c: second_coeff * a_ref[r, c] + third_coeff * v,
        )
        load(lefts, b_ref, count)
        if not last:
            symmetric(t_ref, count, lambda v, r, c: first_coeff * a_ref[r, c] + v)
            load(rights, t_ref, count)
            symmetric(a_ref, count, lambda v, r, c: first_coeff * t_ref[r, c] + v)
        load(rights, x_ref, 2)
        for r in range(4):
            rows = slice(r * 128, (r + 1) * 128)
            value = first_coeff * x_ref[rows, :] + block(rows, slice(0, N), 2)
            if not last:
                x_ref[rows, :] = value
            else:
                update = value * (0.2 * math.sqrt(max(N, 4 * N)))
                update_out[rows, :] = update
                weight = master[rows, :]
                weight = weight - learn_rate * (update + weight_decay * weight)
                master_out[rows, :] = weight
                rounded_out[rows, :] = weight.astype(BF16)

    for r in range(4):
        rows = slice(r * 128, (r + 1) * 128)
        grad = slab[rows, :].astype(F32)
        moment = momentum_decay * mom[rows, :] + grad
        mom_out[rows, :] = moment
        x_ref[rows, :] = (grad + momentum_decay * moment) * factor
        a_ref[rows, :] = a_ref[rows, :] * (factor * factor)

    iterate(3, False)

    def middle(step, carry):
        iterate(2, False)
        return carry

    lax.fori_loop(1, ITERS - 1, middle, 0)
    iterate(2, True)


def ns_call(mom, slab, master, gram):
    vmem = pl.BlockSpec(memory_space=pltpu.VMEM)
    square = jax.ShapeDtypeStruct((N, N), F32)
    return pl.pallas_call(
        ns_kernel,
        out_shape=(square, square, square, jax.ShapeDtypeStruct((N, N), BF16)),
        in_specs=[vmem] * 4,
        out_specs=(vmem,) * 4,
        scratch_shapes=[pltpu.VMEM((N, N), F32)] * 4 + [pltpu.VMEM((N, N), BF16)] * 6,
        compiler_params=pltpu.CompilerParams(vmem_limit_bytes=40 << 20),
        cost_estimate=pl.CostEstimate(
            flops=63 * 2 * N**3, bytes_accessed=7 << 20, transcendentals=0
        ),
        name="newton_schulz",
    )(mom, slab, master, gram)


def rollout_kernel(table, slab, out, *scratch):
    held, chosen = scratch[:CHUNKS], scratch[CHUNKS : 2 * CHUNKS]
    s1_send, s1_recv, up_send, up_recv, down_send, down_recv, s3_send, s3_recv, own_sem = scratch[
        2 * CHUNKS :
    ]
    x, y, z_hi, z_lo, core = place()
    z = z_hi * 2 + z_lo
    mine = y * 2 + core
    slot = z * 8 + mine

    def device(x, y, z, core):
        return ((z % 2) * 2 + core, (y * 4 + z // 2) * 4 + x)

    def in_plane(index):
        return device((index // 2) % 4, index // 8, z, index % 2)

    here = (y * 4 + x) * 2 + core
    above, below = device(x, y, (z + 1) % 8, core), device(x, y, (z + 7) % 8, core)

    barrier = pltpu.get_barrier_semaphore()

    def greet(step, carry):
        pl.semaphore_signal(
            barrier, inc=1, device_id=in_plane((here + step) % 32), device_id_type=MESH
        )
        return carry

    lax.fori_loop(1, 32, greet, 0)
    for to in (above, below):
        pl.semaphore_signal(barrier, inc=1, device_id=to, device_id_type=MESH)
    pl.semaphore_wait(barrier, 33)

    for chunk in range(CHUNKS):
        for step in range(1, 8):
            to = (mine + step) % 8
            rows = pl.ds(pl.multiple_of(to * 64 + chunk * DEPTH, DEPTH), DEPTH)
            pltpu.make_async_remote_copy(
                src_ref=slab.at[rows, :], dst_ref=held[chunk].at[slot],
                send_sem=s1_send.at[chunk], recv_sem=s1_recv.at[chunk],
                device_id=device(x, to // 2, z, to % 2), device_id_type=MESH,
            ).start()
        held[chunk][slot] = slab[pl.ds(pl.multiple_of(mine * 64 + chunk * DEPTH, DEPTH), DEPTH), :]

    def spread(chunk):
        part = held[chunk].at[pl.ds(0, 7)]
        return pltpu.make_async_remote_copy(
            src_ref=part, dst_ref=part, send_sem=s1_send.at[chunk], recv_sem=s1_recv.at[chunk],
            device_id=above, device_id_type=MESH,
        )

    def along(chunk, step, up):
        if up:
            first, count = ((z + 9 - step) % 8) * 8, 8 if step < 4 else 4
            sends, recvs, to = up_send, up_recv, above
        else:
            first, count = ((z + step - 1) % 8) * 8 + (0 if step < 4 else 4), 8 if step < 4 else 4
            sends, recvs, to = down_send, down_recv, below
        part = held[chunk].at[pl.ds(first, count)]
        index = chunk * 4 + step - 1
        return pltpu.make_async_remote_copy(
            src_ref=part, dst_ref=part, send_sem=sends.at[index], recv_sem=recvs.at[index],
            device_id=to, device_id_type=MESH,
        )

    def deliver(chunk):
        rows = pl.ds(pl.multiple_of(mine * 64 + chunk * DEPTH, DEPTH), DEPTH)
        columns = pl.ds(pl.multiple_of(x * N, N), N)
        target = out.at[rows, columns]

        def pick(index):
            group_core = index % 2
            person = (index // 8 * 4 + z_hi) * 4 + (index // 2) % 4
            chosen[chunk][index] = held[chunk][table[group_core, person]]

        def send(step, carry):
            index = (here + step) % 32
            pick(index)
            pltpu.make_async_remote_copy(
                src_ref=chosen[chunk].at[index], dst_ref=target,
                send_sem=s3_send.at[chunk], recv_sem=s3_recv,
                device_id=in_plane(index), device_id_type=MESH,
            ).start()
            return carry

        lax.fori_loop(1, 32, send, 0)
        pick(here)
        pltpu.make_async_copy(chosen[chunk].at[here], target, own_sem.at[chunk]).start()

    order = sorted(
        ((step + 2 * chunk, chunk, step) for chunk in range(CHUNKS) for step in range(1, 5))
    )
    for _, chunk, step in order:
        if step == 1:
            spread(chunk).wait_recv()
        else:
            along(chunk, step - 1, True).wait_recv()
            along(chunk, step - 1, False).wait_recv()
        along(chunk, step, True).start()
        along(chunk, step, False).start()
        if step == 4 and chunk > 0:
            along(chunk - 1, 4, True).wait_recv()
            along(chunk - 1, 4, False).wait_recv()
            deliver(chunk - 1)
    along(CHUNKS - 1, 4, True).wait_recv()
    along(CHUNKS - 1, 4, False).wait_recv()
    deliver(CHUNKS - 1)

    for chunk in range(CHUNKS):
        spread(chunk).wait_send()
        for step in range(1, 5):
            along(chunk, step, True).wait_send()
            along(chunk, step, False).wait_send()
        part = chosen[chunk].at[pl.ds(0, 31)]
        pltpu.make_async_remote_copy(
            src_ref=part, dst_ref=part, send_sem=s3_send.at[chunk], recv_sem=s3_recv,
            device_id=above, device_id_type=MESH,
        ).wait_send()
        rows = pl.ds(pl.multiple_of(mine * 64 + chunk * DEPTH, DEPTH), DEPTH)
        columns = pl.ds(pl.multiple_of(x * N, N), N)
        pltpu.make_async_copy(
            chosen[chunk].at[here], out.at[rows, columns], own_sem.at[chunk]
        ).wait()
    arrived = out.at[pl.ds(0, 31 * 16), :]
    pltpu.make_async_remote_copy(
        src_ref=arrived, dst_ref=arrived, send_sem=s3_send.at[0], recv_sem=s3_recv,
        device_id=above, device_id_type=MESH,
    ).wait_recv()


def rollout_call(table, slab):
    dma = pltpu.SemaphoreType.DMA
    steps = dma((CHUNKS * 4,))
    return pl.pallas_call(
        rollout_kernel,
        out_shape=jax.ShapeDtypeStruct((N, 4 * N), BF16),
        in_specs=[
            pl.BlockSpec(memory_space=pltpu.SMEM),
            pl.BlockSpec(memory_space=pltpu.VMEM),
        ],
        out_specs=pl.BlockSpec(memory_space=pl.ANY),
        scratch_shapes=[pltpu.VMEM((64, DEPTH, N), BF16)] * CHUNKS
        + [pltpu.VMEM((32, DEPTH, N), BF16)] * CHUNKS
        + [dma((CHUNKS,)), dma((CHUNKS,)), steps, steps, steps, steps, dma((CHUNKS,)), dma, dma((CHUNKS,))],
        compiler_params=pltpu.CompilerParams(
            collective_id=1, has_side_effects=True, vmem_limit_bytes=40 << 20
        ),
        name="rollout",
    )(table, slab)


def slots(owned_matrix, rollout_matrix):
    core = lax.axis_index("grp") % 2
    theirs = lax.ppermute(rollout_matrix, "grp", [(0, 1), (1, 0), (2, 3), (3, 2)])
    own = jnp.arange(2, dtype=jnp.int32)[:, None] == core
    wanted = jnp.where(own, rollout_matrix, theirs)
    owner = jnp.arange(4 * QUADS, dtype=jnp.int32)
    group, quad = owner // QUADS, owner % QUADS
    identity = group * QUADS + owned_matrix.reshape(-1)
    slot = ((quad % 4) * 2 + group // 2) * 8 + (quad // 4) * 2 + group % 2
    match = wanted[:, :, None] == identity[None, None, :]
    return jnp.sum(jnp.where(match, slot[None, None, :], 0), axis=2)


def shards(gradient, momentum, master_weight, owned_matrix, rollout_matrix):
    table = slots(owned_matrix, rollout_matrix)
    slab, gram = gram_call(owned_matrix, gradient, momentum[0])
    moment, update, weight, rounded = ns_call(momentum[0], slab, master_weight[0], gram)
    rollout = rollout_call(table, rounded)
    return (moment[None], update[None], weight[None], rollout[None])


def solution(mesh):
    everyone = P(("grp", "dev"), None, None)
    return jax.shard_map(
        shards,
        mesh=mesh,
        in_specs=(P("grp", "dev", None), everyone, everyone, P(), P("grp", None)),
        out_specs=(everyone,) * 4,
        check_vma=False,
    )
```

```python
import math

import jax
import jax.numpy as jnp
from jax import lax
from jax.experimental import pallas as pl
from jax.experimental.pallas import tpu as pltpu
from jax.sharding import PartitionSpec as P

MESH = pl.DeviceIdType.MESH
F32 = jnp.float32
BF16 = jnp.bfloat16

ITERS = 5
momentum_decay = 0.95
learn_rate = 0.02
weight_decay = 0.1
first_coeff = 3.4445
second_coeff = -4.775
third_coeff = 2.0315
norm_epsilon = 1e-07

N = 512
HALF = 256
QUADS = 16
DEVS = 64
CHUNKS = 8
DEPTH = 16
TILES = [(i, j) for i in range(4) for j in range(i, 4)]
PIECE = len(TILES) * 128 // 4


def split2(value):
    high = value.astype(BF16)
    return high, (value - high.astype(F32)).astype(BF16)


def split3(value):
    high = value.astype(BF16)
    rest = value - high.astype(F32)
    mid = rest.astype(BF16)
    return high, mid, (rest - mid.astype(F32)).astype(BF16)


def dot(left, right):
    return jnp.dot(left, right, preferred_element_type=F32)


def dot_t(left, right):
    return lax.dot_general(left, right, (((1,), (1,)), ((), ())), preferred_element_type=F32)


def terms(count):
    pairs = [(i, j) for i in range(count) for j in range(count) if i + j < count]
    return sorted(pairs, key=lambda pair: -sum(pair))


SCHEDULE = [
    (int(step[0]), int(step[1]))
    for step in (
        "01 11 31 21 41 12 02 32 51 13 22 03 42 14 33 61 04 23 10 34 52 71 00 43 24 30 62 53 44 72"
        " 20 63 54 40 73 64 50 74 60 70"
    ).split(" ")
]


def blocks_of(unit):
    return unit // 5, slice(unit % 5 * 64, (unit % 5 + 1) * 64)


def kernel(
    owned, wanted, grad_in, mom_in, master_in,
    mom_out, update_out, master_out, rollout_out,
    grad, mom, master, update,
    outbox, inbox, partial, others, full,
    a_ref, b_ref, t_ref, x_ref, p0, p1, p2, q0, q1, q2,
    rounded, chosen, names, table_v, table,
    in_sem, out_sem, names_send, names_recv, table_sem,
    send_sem, recv_sem, rs_send, rs_recv, ag_send, ag_recv,
    s1_send, s1_recv, up_send, up_recv, down_send, down_recv, s3_send, s3_recv, own_sem,
    *held,
):
    grp, dev = lax.axis_index("grp"), lax.axis_index("dev")
    x, z_hi, y = lax.rem(dev, 4), lax.rem(lax.div(dev, 4), 4), lax.div(dev, 16)
    z_lo, core = lax.div(grp, 2), lax.rem(grp, 2)
    z = z_hi * 2 + z_lo
    mine = y * 2 + core
    slot = z * 8 + mine

    def device(x, y, z, core):
        return (lax.rem(z, 2) * 2 + core, (y * 4 + lax.div(z, 2)) * 4 + x)

    def in_plane(index):
        across, along_y = lax.rem(lax.div(index, 2), 4), lax.div(index, 8)
        return (z_lo * 2 + lax.rem(index, 2), (along_y * 4 + z_hi) * 4 + across)

    here = (y * 4 + x) * 2 + core
    above, below = device(x, y, lax.rem(z + 1, 8), core), device(x, y, lax.rem(z + 7, 8), core)
    twin = (z_lo * 2 + 1 - core, dev)

    def remote(src, dst, sends, recvs, to):
        return pltpu.make_async_remote_copy(
            src_ref=src, dst_ref=dst, send_sem=sends, recv_sem=recvs, device_id=to, device_id_type=MESH
        )

    loads = [
        pltpu.make_async_copy(src, dst, in_sem.at[index])
        for index, (src, dst) in enumerate(
            ((grad_in, grad), (mom_in, mom), (master_in, master))
        )
    ]
    for copy in loads:
        copy.start()

    barrier = pltpu.get_barrier_semaphore()

    def greet(to):
        pl.semaphore_signal(barrier, inc=1, device_id=to, device_id_type=MESH)

    def greet_group(step, carry):
        greet((grp, lax.rem(dev + step, DEVS)))
        return carry

    def greet_plane(step, carry):
        greet((z_lo * 2 + 1 - core, in_plane(2 * step)[1]))
        return carry

    lax.fori_loop(1, DEVS, greet_group, 0)
    lax.fori_loop(0, 16, greet_plane, 0)
    greet(above)
    greet(below)

    names[0] = jnp.zeros((8, 128), jnp.int32)
    names[0, 0:1, 0:DEVS] = wanted[...]
    loads[0].wait()

    def fill(q, carry):
        rows = grad[owned[grp, q]].astype(F32)
        for c in range(4):
            left = rows[:, c * N : c * N + HALF]
            right = rows[:, c * N + HALF : (c + 1) * N]
            outbox[q * 4 + c] = jnp.concatenate([left, right], axis=0).astype(BF16)
        return carry

    lax.fori_loop(0, QUADS, fill, 0)
    pl.semaphore_wait(barrier, DEVS - 1 + 18)

    def send(step, carry):
        to = lax.rem(dev + step, DEVS)
        remote(outbox.at[to], inbox.at[dev], send_sem, recv_sem, (grp, to)).start()
        return carry

    lax.fori_loop(1, DEVS, send, 0)
    tell = remote(names.at[0], names.at[1], names_send, names_recv, twin)
    tell.start()
    inbox[dev] = outbox[dev]

    tell.wait_recv()
    found = [jnp.zeros((8, 128), jnp.int32), jnp.zeros((8, 128), jnp.int32)]
    own_names, twin_names = names[0], names[1]
    for group in range(4):
        for quad in range(QUADS):
            identity = group * QUADS + owned[group, quad]
            at = ((quad % 4) * 2 + group // 2) * 8 + (quad // 4) * 2 + group % 2
            found[0] = jnp.where(own_names == identity, at, found[0])
            found[1] = jnp.where(twin_names == identity, at, found[1])
    table_v[core] = found[0]
    table_v[1 - core] = found[1]
    lookup = pltpu.make_async_copy(table_v, table, table_sem)
    lookup.start()

    loads[1].wait()
    rest = pl.ds(0, DEVS - 1)
    everything = remote(
        outbox.at[rest], inbox.at[rest], send_sem, recv_sem, (grp, lax.rem(dev + 1, DEVS))
    )
    everything.wait_recv()

    lefts, rights = (p0, p1, p2), (q0, q1, q2)
    for r in range(4):
        got = inbox[pl.ds(r * 16, 16)].astype(F32)
        slab = jnp.concatenate(
            [got[:, :8, :].reshape(128, HALF), got[:, 8:, :].reshape(128, HALF)], axis=1
        )
        rows = slice(r * 128, (r + 1) * 128)
        moment = momentum_decay * mom[rows, :] + slab
        mom[rows, :] = moment
        nesterov = slab + momentum_decay * moment
        x_ref[rows, :] = nesterov
        for left, part in zip(lefts, split3(nesterov)):
            left[rows, :] = part
    stores = [pltpu.make_async_copy(mom, mom_out, out_sem.at[0])]
    stores[0].start()

    at = 0
    for i in range(4):
        total = None
        for a, b in terms(3):
            term = dot_t(lefts[a][i * 128 : (i + 1) * 128, :], lefts[b][i * 128 :, :])
            total = term if total is None else total + term
        for j in range(4 - i):
            for h in range(2):
                piece, rows = blocks_of(2 * at + h)
                partial[piece, rows, :] = total[h * 64 : (h + 1) * 64, j * 128 : (j + 1) * 128]
            at += 1

    def share(step, src, dst, sends, recvs):
        to = (grp, dev - x + lax.rem(x + step, 4))
        return remote(src, dst, sends.at[step - 1], recvs.at[step - 1], to)

    scatter = [
        share(step, partial.at[lax.rem(x + step, 4)], others.at[step - 1], rs_send, rs_recv)
        for step in (2, 1, 3)
    ]
    for copy in scatter:
        copy.start()
    for copy in scatter:
        copy.wait_recv()
    full[x] = (partial[x] + others[0]) + (others[1] + others[2])
    gather = [share(step, full.at[x], full.at[x], ag_send, ag_recv) for step in (2, 1, 3)]
    for copy in gather:
        copy.start()
    for copy in gather:
        copy.wait_recv()

    trace = None
    for at, (i, j) in enumerate(TILES):
        halves = [blocks_of(2 * at + h) for h in range(2)]
        tile = jnp.concatenate([full[piece, rows, :] for piece, rows in halves], axis=0)
        a_ref[i * 128 : (i + 1) * 128, j * 128 : (j + 1) * 128] = tile
        if i != j:
            a_ref[j * 128 : (j + 1) * 128, i * 128 : (i + 1) * 128] = tile.T
        else:
            row = lax.broadcasted_iota(jnp.int32, (128, 128), 0)
            col = lax.broadcasted_iota(jnp.int32, (128, 128), 1)
            diagonal = jnp.where(row == col, tile, 0.0)
            trace = diagonal if trace is None else trace + diagonal
    trace = jnp.sum(jnp.sum(trace, axis=0, keepdims=True), axis=1, keepdims=True)
    factor = 1.0 / (jnp.sqrt(trace) + norm_epsilon)
    for r in range(4):
        rows = slice(r * 128, (r + 1) * 128)
        x_ref[rows, :] = x_ref[rows, :] * factor
        a_ref[rows, :] = a_ref[rows, :] * (factor * factor)

    def load(slots, value_ref, count):
        for r in range(4):
            rows = slice(r * 128, (r + 1) * 128)
            value = value_ref[rows, :]
            for part_ref, part in zip(slots, split2(value) if count == 2 else split3(value)):
                part_ref[rows, :] = part

    def block(rows, cols, count):
        total = None
        for a, b in terms(count):
            term = dot(lefts[a][rows, :], rights[b][:, cols])
            total = term if total is None else total + term
        return total

    everywhere, high = slice(0, N), slice(HALF, N)

    def symmetric(dst, count, finish):
        for r in range(4):
            rows = slice(r * 128, (r + 1) * 128)
            cols = everywhere if r < 2 else high
            dst[rows, cols] = finish(block(rows, cols, count), rows, cols)
        for r in range(2):
            for s in range(2, 4):
                dst[s * 128 : (s + 1) * 128, r * 128 : (r + 1) * 128] = dst[
                    r * 128 : (r + 1) * 128, s * 128 : (s + 1) * 128
                ].T

    def iterate(count):
        load(lefts, a_ref, count)
        load(rights, a_ref, count)
        symmetric(b_ref, count, lambda v, r, c: second_coeff * a_ref[r, c] + third_coeff * v)
        load(lefts, b_ref, count)
        symmetric(t_ref, count, lambda v, r, c: first_coeff * a_ref[r, c] + v)
        load(rights, t_ref, count)
        symmetric(a_ref, count, lambda v, r, c: first_coeff * t_ref[r, c] + v)
        load(rights, x_ref, 2)
        for r in range(4):
            rows = slice(r * 128, (r + 1) * 128)
            x_ref[rows, :] = first_coeff * x_ref[rows, :] + block(rows, everywhere, 2)

    iterate(3)
    iterate(3)

    def middle(step, carry):
        iterate(2)
        return carry

    lax.fori_loop(2, ITERS - 1, middle, 0)

    def region(chunk, part):
        first = chunk // 2 * 128 + part * DEPTH
        return pl.ds(pl.multiple_of(first, DEPTH), DEPTH), slice(chunk % 2 * HALF, (chunk % 2 + 1) * HALF)

    def spread(chunk):
        part = held[chunk].at[pl.ds(0, 7)]
        return remote(part, part, s1_send.at[chunk], s1_recv.at[chunk], above)

    loads[2].wait()
    load(lefts, a_ref, 2)
    load(rights, a_ref, 2)
    x_high, x_low = x_parts = (p2, q2)
    for r in range(4):
        rows = slice(r * 128, (r + 1) * 128)
        value = x_ref[rows, :]
        for part_ref, part in zip(x_parts, split2(value)):
            part_ref[rows, :] = part
    for r in range(4):
        rows = slice(r * 128, (r + 1) * 128)
        mixed = second_coeff * a_ref[rows, :] + third_coeff * block(rows, everywhere, 2)
        mixed_high, mixed_low = split2(mixed)
        value = (
            dot(mixed_high, x_low[...]) + dot(mixed_low, x_high[...])
        ) + dot(mixed_high, x_high[...])
        step = (first_coeff * x_ref[rows, :] + value) * (0.2 * math.sqrt(max(N, 4 * N)))
        update[rows, :] = step
        weight = master[rows, :]
        weight = weight - learn_rate * (step + weight_decay * weight)
        master[rows, :] = weight
        rounded[rows, :] = weight.astype(BF16)
        for chunk in (2 * r, 2 * r + 1):
            for away in range(1, 8):
                to = lax.rem(mine + away, 8)
                remote(
                    rounded.at[region(chunk, to)], held[chunk].at[slot],
                    s1_send.at[chunk], s1_recv.at[chunk],
                    device(x, lax.div(to, 2), z, lax.rem(to, 2)),
                ).start()
            held[chunk][slot] = rounded[region(chunk, mine)]
    stores += [
        pltpu.make_async_copy(update, update_out, out_sem.at[1]),
        pltpu.make_async_copy(master, master_out, out_sem.at[2]),
    ]
    stores[1].start()
    stores[2].start()
    lookup.wait()

    def along(chunk, step, up):
        count = 8 if step < 4 else 4
        plane = lax.rem(z + 9 - step, 8) if up else lax.rem(z + step - 1, 8)
        first = plane * 8 + (0 if up or step < 4 else 4)
        part = held[chunk].at[pl.ds(first, count)]
        index = chunk * 4 + step - 1
        if up:
            return remote(part, part, up_send.at[index], up_recv.at[index], above)
        return remote(part, part, down_send.at[index], down_recv.at[index], below)

    def goal(chunk):
        first = x * N + chunk % 2 * HALF
        return rollout_out.at[region(chunk, mine)[0], pl.ds(pl.multiple_of(first, HALF), HALF)]

    def pick(chunk, index):
        chosen[chunk, index] = held[chunk][table[lax.rem(index, 2), 0, in_plane(index)[1]]]

    def deliver(chunk):
        target = goal(chunk)

        def give(step, carry):
            index = lax.rem(here + step, 32)
            pick(chunk, index)
            remote(
                chosen.at[chunk, index], target, s3_send.at[chunk], s3_recv, in_plane(index)
            ).start()
            return carry

        lax.fori_loop(1, 32, give, 0)
        pick(chunk, here)
        pltpu.make_async_copy(chosen.at[chunk, here], target, own_sem.at[chunk]).start()

    for chunk, step in SCHEDULE:
        if step == 1:
            spread(chunk).wait_recv()
        else:
            hop = step - 1 if step else 4
            along(chunk, hop, True).wait_recv()
            along(chunk, hop, False).wait_recv()
        if step:
            along(chunk, step, True).start()
            along(chunk, step, False).start()
        else:
            deliver(chunk)

    tell.wait_send()
    everything.wait_send()
    for copy in scatter + gather:
        copy.wait_send()
    for copy in stores:
        copy.wait()
    for chunk in range(CHUNKS):
        spread(chunk).wait_send()
        for step in range(1, 5):
            along(chunk, step, True).wait_send()
            along(chunk, step, False).wait_send()
        part = chosen.at[chunk, pl.ds(0, 31)]
        remote(part, part, s3_send.at[chunk], s3_recv, above).wait_send()
        pltpu.make_async_copy(chosen.at[chunk, here], goal(chunk), own_sem.at[chunk]).wait()
    arrived = rollout_out.at[pl.ds(0, 31 * 16), :]
    remote(arrived, arrived, s3_send.at[0], s3_recv, above).wait_recv()


def shards(gradient, momentum, master_weight, owned_matrix, rollout_matrix):
    smem, vmem, anywhere = (
        pl.BlockSpec(memory_space=space) for space in (pltpu.SMEM, pltpu.VMEM, pl.ANY)
    )
    dma = pltpu.SemaphoreType.DMA
    square = jax.ShapeDtypeStruct((N, N), F32)
    wide, half = pltpu.VMEM((N, N), F32), pltpu.VMEM((N, N), BF16)
    hops = dma((CHUNKS * 4,))
    box = pltpu.VMEM((DEVS, 16, HALF), BF16)
    moment, update, weight, rollout = pl.pallas_call(
        kernel,
        out_shape=(square, square, square, jax.ShapeDtypeStruct((N, 4 * N), BF16)),
        in_specs=[smem, vmem, anywhere, anywhere, anywhere],
        out_specs=(anywhere,) * 4,
        scratch_shapes=[pltpu.VMEM((QUADS, 8, 4 * N), BF16), wide, wide, wide]
        + [box, box]
        + [pltpu.VMEM((count, PIECE, 128), F32) for count in (4, 3, 4)]
        + [wide] * 4
        + [half] * 6
        + [
            half,
            pltpu.VMEM((CHUNKS, 32, DEPTH, HALF), BF16),
            pltpu.VMEM((2, 8, 128), jnp.int32),
            pltpu.VMEM((2, 8, 128), jnp.int32),
            pltpu.SMEM((2, 8, 128), jnp.int32),
        ]
        + [dma((3,)), dma((3,)), dma, dma, dma]
        + [dma, dma, dma((3,)), dma((3,)), dma((3,)), dma((3,))]
        + [dma((CHUNKS,)), dma((CHUNKS,)), hops, hops, hops, hops, dma((CHUNKS,)), dma, dma((CHUNKS,))]
        + [pltpu.VMEM((64, DEPTH, HALF), BF16)] * CHUNKS,
        compiler_params=pltpu.CompilerParams(
            collective_id=0, has_side_effects=True, vmem_limit_bytes=63 << 20
        ),
        name="muon",
    )(owned_matrix, rollout_matrix, gradient, momentum[0], master_weight[0])
    return (moment[None], update[None], weight[None], rollout[None])


def solution(mesh):
    everyone = P(("grp", "dev"), None, None)
    return jax.shard_map(
        shards,
        mesh=mesh,
        in_specs=(P("grp", "dev", None), everyone, everyone, P(), P("grp", None)),
        out_specs=(everyone,) * 4,
        check_vma=False,
    )
```

```python
import math

import jax
import jax.numpy as jnp
from jax import lax
from jax.experimental import pallas as pl
from jax.experimental.pallas import tpu as pltpu
from jax.sharding import PartitionSpec as P

MESH = pl.DeviceIdType.MESH
F32 = jnp.float32
BF16 = jnp.bfloat16

ITERS = 5
momentum_decay = 0.95
learn_rate = 0.02
weight_decay = 0.1
first_coeff = 3.4445
second_coeff = -4.775
third_coeff = 2.0315
norm_epsilon = 1e-07

N = 512
HALF = 256
QUADS = 16
DEVS = 64
CHUNKS = 8
DEPTH = 16
TILES = [(i, j) for i in range(4) for j in range(i, 4)]
PIECE = len(TILES) * 128 // 4


def split2(value):
    high = value.astype(BF16)
    return high, (value - high.astype(F32)).astype(BF16)


def split3(value):
    high = value.astype(BF16)
    rest = value - high.astype(F32)
    mid = rest.astype(BF16)
    return high, mid, (rest - mid.astype(F32)).astype(BF16)


def dot(left, right):
    return jnp.dot(left, right, preferred_element_type=F32)


def dot_t(left, right):
    return lax.dot_general(left, right, (((1,), (1,)), ((), ())), preferred_element_type=F32)


def terms(count):
    pairs = [(i, j) for i in range(count) for j in range(count) if i + j < count]
    return sorted(pairs, key=lambda pair: -sum(pair))


SCHEDULE = [
    1, 11, 31, 21, 41, 12, 2, 32, 51, 13, 22, 3, 42, 14, 33, 61, 4, 23, 10, 34,
    52, 71, 0, 43, 24, 30, 62, 53, 44, 72, 20, 63, 54, 40, 73, 64, 50, 74, 60, 70,
]


def blocks_of(unit):
    return unit // 5, slice(unit % 5 * 64, (unit % 5 + 1) * 64)


def kernel(
    owned, wanted, grad_in, mom_in, master_in,
    mom_out, update_out, master_out, rollout_out,
    grad, mom, master, update,
    outbox, inbox, partial, others, full,
    a_ref, t_ref, x_ref,
    a0, a1, a2, b0, b1, b2, t0, t1, t2, x0, x1, x2, x3,
    rounded, chosen, names, table_v, table,
    in_sem, out_sem, names_send, names_recv, table_sem,
    send_sem, recv_sem, rs_send, rs_recv, ag_send, ag_recv,
    s1_send, s1_recv, up_send, up_recv, down_send, down_recv, s3_send, s3_recv, own_sem,
    *held,
):
    grp, dev = lax.axis_index("grp"), lax.axis_index("dev")
    x, z_hi, y = lax.rem(dev, 4), lax.rem(lax.div(dev, 4), 4), lax.div(dev, 16)
    z_lo, core = lax.div(grp, 2), lax.rem(grp, 2)
    z = z_hi * 2 + z_lo
    mine = y * 2 + core
    slot = z * 8 + mine

    def device(x, y, z, core):
        return (lax.rem(z, 2) * 2 + core, (y * 4 + lax.div(z, 2)) * 4 + x)

    def in_plane(index):
        across, along_y = lax.rem(lax.div(index, 2), 4), lax.div(index, 8)
        return (z_lo * 2 + lax.rem(index, 2), (along_y * 4 + z_hi) * 4 + across)

    here = (y * 4 + x) * 2 + core
    above, below = device(x, y, lax.rem(z + 1, 8), core), device(x, y, lax.rem(z + 7, 8), core)
    twin = (z_lo * 2 + 1 - core, dev)

    def remote(src, dst, sends, recvs, to):
        return pltpu.make_async_remote_copy(
            src_ref=src, dst_ref=dst, send_sem=sends, recv_sem=recvs, device_id=to, device_id_type=MESH
        )

    loads = [
        pltpu.make_async_copy(src, dst, in_sem.at[index])
        for index, (src, dst) in enumerate(
            ((grad_in, grad), (mom_in, mom), (master_in, master))
        )
    ]
    for copy in loads:
        copy.start()

    barrier = pltpu.get_barrier_semaphore()

    def greet(to):
        pl.semaphore_signal(barrier, inc=1, device_id=to, device_id_type=MESH)

    def greet_group(step, carry):
        greet((grp, lax.rem(dev + step, DEVS)))
        return carry

    def greet_plane(step, carry):
        greet((z_lo * 2 + 1 - core, in_plane(2 * step)[1]))
        return carry

    lax.fori_loop(1, DEVS, greet_group, 0)
    lax.fori_loop(0, 16, greet_plane, 0)
    greet(above)
    greet(below)

    names[0] = jnp.zeros((8, 128), jnp.int32)
    names[0, 0:1, 0:DEVS] = wanted[...]
    loads[0].wait()

    def fill(q, carry):
        rows = grad[owned[grp, q]].astype(F32)
        for c in range(4):
            left = rows[:, c * N : c * N + HALF]
            right = rows[:, c * N + HALF : (c + 1) * N]
            outbox[q * 4 + c] = jnp.concatenate([left, right], axis=0).astype(BF16)
        return carry

    lax.fori_loop(0, QUADS, fill, 0)
    pl.semaphore_wait(barrier, DEVS - 1 + 18)

    def send(step, carry):
        to = lax.rem(dev + step, DEVS)
        remote(outbox.at[to], inbox.at[dev], send_sem, recv_sem, (grp, to)).start()
        return carry

    lax.fori_loop(1, DEVS, send, 0)
    tell = remote(names.at[0], names.at[1], names_send, names_recv, twin)
    tell.start()
    inbox[dev] = outbox[dev]

    tell.wait_recv()
    found = [jnp.zeros((8, 128), jnp.int32), jnp.zeros((8, 128), jnp.int32)]
    own_names, twin_names = names[0], names[1]
    for group in range(4):
        for quad in range(QUADS):
            identity = group * QUADS + owned[group, quad]
            at = ((quad % 4) * 2 + group // 2) * 8 + (quad // 4) * 2 + group % 2
            found[0] = jnp.where(own_names == identity, at, found[0])
            found[1] = jnp.where(twin_names == identity, at, found[1])
    table_v[core] = found[0]
    table_v[1 - core] = found[1]
    lookup = pltpu.make_async_copy(table_v, table, table_sem)
    lookup.start()

    loads[1].wait()
    rest = pl.ds(0, DEVS - 1)
    everything = remote(
        outbox.at[rest], inbox.at[rest], send_sem, recv_sem, (grp, lax.rem(dev + 1, DEVS))
    )
    everything.wait_recv()

    a_parts, b_parts, t_parts = (a0, a1, a2), (b0, b1, b2), (t0, t1, t2)
    x_parts = ((x0, x1), (x2, x3))
    for r in range(4):
        got = inbox[pl.ds(r * 16, 16)].astype(F32)
        slab = jnp.concatenate(
            [got[:, :8, :].reshape(128, HALF), got[:, 8:, :].reshape(128, HALF)], axis=1
        )
        rows = slice(r * 128, (r + 1) * 128)
        moment = momentum_decay * mom[rows, :] + slab
        mom[rows, :] = moment
        nesterov = slab + momentum_decay * moment
        x_ref[rows, :] = nesterov
        for part_ref, part in zip(b_parts, split3(nesterov)):
            part_ref[rows, :] = part
    stores = [pltpu.make_async_copy(mom, mom_out, out_sem.at[0])]
    stores[0].start()

    at = 0
    for i in range(4):
        total = None
        for a, b in terms(3):
            term = dot_t(b_parts[a][i * 128 : (i + 1) * 128, :], b_parts[b][i * 128 :, :])
            total = term if total is None else total + term
        for j in range(4 - i):
            for h in range(2):
                piece, rows = blocks_of(2 * at + h)
                partial[piece, rows, :] = total[h * 64 : (h + 1) * 64, j * 128 : (j + 1) * 128]
            at += 1

    def share(step, src, dst, sends, recvs):
        to = (grp, dev - x + lax.rem(x + step, 4))
        return remote(src, dst, sends.at[step - 1], recvs.at[step - 1], to)

    scatter = [
        share(step, partial.at[lax.rem(x + step, 4)], others.at[step - 1], rs_send, rs_recv)
        for step in (2, 1, 3)
    ]
    for copy in scatter:
        copy.start()
    for copy in scatter:
        copy.wait_recv()
    full[x] = (partial[x] + others[0]) + (others[1] + others[2])
    gather = [share(step, full.at[x], full.at[x], ag_send, ag_recv) for step in (2, 1, 3)]
    for copy in gather:
        copy.start()
    for copy in gather:
        copy.wait_recv()

    trace = None
    for at, (i, j) in enumerate(TILES):
        halves = [blocks_of(2 * at + h) for h in range(2)]
        tile = jnp.concatenate([full[piece, rows, :] for piece, rows in halves], axis=0)
        a_ref[i * 128 : (i + 1) * 128, j * 128 : (j + 1) * 128] = tile
        if i != j:
            a_ref[j * 128 : (j + 1) * 128, i * 128 : (i + 1) * 128] = tile.T
        else:
            row = lax.broadcasted_iota(jnp.int32, (128, 128), 0)
            col = lax.broadcasted_iota(jnp.int32, (128, 128), 1)
            diagonal = jnp.where(row == col, tile, 0.0)
            trace = diagonal if trace is None else trace + diagonal
    trace = jnp.sum(jnp.sum(trace, axis=0, keepdims=True), axis=1, keepdims=True)
    factor = 1.0 / (jnp.sqrt(trace) + norm_epsilon)
    everywhere, high = slice(0, N), slice(HALF, N)

    def emit(value, rows, cols, whole, parts):
        if whole is not None:
            whole[rows, cols] = value
        for part_ref, part in zip(parts, split2(value) if len(parts) == 2 else split3(value)):
            part_ref[rows, cols] = part

    for r in range(4):
        rows = slice(r * 128, (r + 1) * 128)
        emit(x_ref[rows, :] * factor, rows, everywhere, x_ref, x_parts[0])
        emit(a_ref[rows, :] * (factor * factor), rows, everywhere, a_ref, a_parts)

    def block(lefts, rights, rows, cols, count):
        total = None
        for a, b in terms(count):
            term = dot(lefts[a][rows, :], rights[b][:, cols])
            total = term if total is None else total + term
        return total

    def symmetric(lefts, rights, count, finish, whole, parts):
        for r in range(4):
            rows = slice(r * 128, (r + 1) * 128)
            cols = everywhere if r < 2 else high
            value = finish(block(lefts, rights, rows, cols, count), rows, cols)
            emit(value, rows, cols, whole, parts)
            if r < 2:
                for s in range(2, 4):
                    mirror = slice(s * 128, (s + 1) * 128)
                    emit(value[:, mirror].T, mirror, rows, whole, parts)

    def iterate(step, count, following):
        symmetric(
            a_parts, a_parts, count,
            lambda v, r, c: second_coeff * a_ref[r, c] + third_coeff * v,
            None, b_parts[:count],
        )
        symmetric(
            b_parts, a_parts, count,
            lambda v, r, c: first_coeff * a_ref[r, c] + v,
            t_ref, t_parts[:count],
        )
        symmetric(
            b_parts, t_parts, count,
            lambda v, r, c: first_coeff * t_ref[r, c] + v,
            a_ref, a_parts[:following],
        )
        for r in range(4):
            rows = slice(r * 128, (r + 1) * 128)
            value = block(b_parts, x_parts[step % 2], rows, everywhere, 2)
            value = first_coeff * x_ref[rows, :] + value
            emit(value, rows, everywhere, x_ref, x_parts[(step + 1) % 2])

    for step, counts in enumerate(((3, 3), (3, 2), (2, 2), (2, 2))):
        iterate(step, *counts)

    def region(chunk, part):
        first = chunk // 2 * 128 + part * DEPTH
        return pl.ds(pl.multiple_of(first, DEPTH), DEPTH), slice(chunk % 2 * HALF, (chunk % 2 + 1) * HALF)

    def spread(chunk):
        part = held[chunk].at[pl.ds(0, 7)]
        return remote(part, part, s1_send.at[chunk], s1_recv.at[chunk], above)

    loads[2].wait()
    for r in range(4):
        rows = slice(r * 128, (r + 1) * 128)
        value = block(a_parts, a_parts, rows, everywhere, 2)
        emit(second_coeff * a_ref[rows, :] + third_coeff * value, rows, everywhere, None, b_parts[:2])
        value = block(b_parts, x_parts[0], rows, everywhere, 2)
        step = (first_coeff * x_ref[rows, :] + value) * (0.2 * math.sqrt(max(N, 4 * N)))
        update[rows, :] = step
        weight = master[rows, :]
        weight = weight - learn_rate * (step + weight_decay * weight)
        master[rows, :] = weight
        rounded[rows, :] = weight.astype(BF16)
        for chunk in (2 * r, 2 * r + 1):
            for away in range(1, 8):
                to = lax.rem(mine + away, 8)
                remote(
                    rounded.at[region(chunk, to)], held[chunk].at[slot],
                    s1_send.at[chunk], s1_recv.at[chunk],
                    device(x, lax.div(to, 2), z, lax.rem(to, 2)),
                ).start()
            held[chunk][slot] = rounded[region(chunk, mine)]
    stores += [
        pltpu.make_async_copy(update, update_out, out_sem.at[1]),
        pltpu.make_async_copy(master, master_out, out_sem.at[2]),
    ]
    stores[1].start()
    stores[2].start()
    lookup.wait()

    def along(chunk, step, up):
        count = 8 if step < 4 else 4
        plane = lax.rem(z + 9 - step, 8) if up else lax.rem(z + step - 1, 8)
        first = plane * 8 + (0 if up or step < 4 else 4)
        part = held[chunk].at[pl.ds(first, count)]
        index = chunk * 4 + step - 1
        if up:
            return remote(part, part, up_send.at[index], up_recv.at[index], above)
        return remote(part, part, down_send.at[index], down_recv.at[index], below)

    def goal(chunk):
        first = x * N + chunk % 2 * HALF
        return rollout_out.at[region(chunk, mine)[0], pl.ds(pl.multiple_of(first, HALF), HALF)]

    def pick(chunk, index):
        chosen[chunk, index] = held[chunk][table[lax.rem(index, 2), 0, in_plane(index)[1]]]

    def deliver(chunk):
        target = goal(chunk)

        def give(step, carry):
            index = lax.rem(here + step, 32)
            pick(chunk, index)
            remote(
                chosen.at[chunk, index], target, s3_send.at[chunk], s3_recv, in_plane(index)
            ).start()
            return carry

        lax.fori_loop(1, 32, give, 0)
        pick(chunk, here)
        pltpu.make_async_copy(chosen.at[chunk, here], target, own_sem.at[chunk]).start()

    for code in SCHEDULE:
        chunk, step = code // 10, code % 10
        if step == 1:
            spread(chunk).wait_recv()
        else:
            hop = step - 1 if step else 4
            along(chunk, hop, True).wait_recv()
            along(chunk, hop, False).wait_recv()
        if step:
            along(chunk, step, True).start()
            along(chunk, step, False).start()
        else:
            deliver(chunk)

    tell.wait_send()
    everything.wait_send()
    for copy in scatter + gather:
        copy.wait_send()
    for copy in stores:
        copy.wait()
    for chunk in range(CHUNKS):
        spread(chunk).wait_send()
        for step in range(1, 5):
            along(chunk, step, True).wait_send()
            along(chunk, step, False).wait_send()
        part = chosen.at[chunk, pl.ds(0, 31)]
        remote(part, part, s3_send.at[chunk], s3_recv, above).wait_send()
        pltpu.make_async_copy(chosen.at[chunk, here], goal(chunk), own_sem.at[chunk]).wait()
    arrived = rollout_out.at[pl.ds(0, 31 * 16), :]
    remote(arrived, arrived, s3_send.at[0], s3_recv, above).wait_recv()


def shards(gradient, momentum, master_weight, owned_matrix, rollout_matrix):
    smem, vmem, anywhere = (
        pl.BlockSpec(memory_space=space) for space in (pltpu.SMEM, pltpu.VMEM, pl.ANY)
    )
    dma = pltpu.SemaphoreType.DMA
    square = jax.ShapeDtypeStruct((N, N), F32)
    wide, half = pltpu.VMEM((N, N), F32), pltpu.VMEM((N, N), BF16)
    hops = dma((CHUNKS * 4,))
    box = pltpu.VMEM((DEVS, 16, HALF), BF16)
    moment, update, weight, rollout = pl.pallas_call(
        kernel,
        out_shape=(square, square, square, jax.ShapeDtypeStruct((N, 4 * N), BF16)),
        in_specs=[smem, vmem, anywhere, anywhere, anywhere],
        out_specs=(anywhere,) * 4,
        scratch_shapes=[pltpu.VMEM((QUADS, 8, 4 * N), BF16), wide, wide, wide]
        + [box, box]
        + [pltpu.VMEM((count, PIECE, 128), F32) for count in (4, 3, 4)]
        + [wide] * 3
        + [half] * 13
        + [
            half,
            pltpu.VMEM((CHUNKS, 32, DEPTH, HALF), BF16),
            pltpu.VMEM((2, 8, 128), jnp.int32),
            pltpu.VMEM((2, 8, 128), jnp.int32),
            pltpu.SMEM((2, 8, 128), jnp.int32),
        ]
        + [dma((3,)), dma((3,)), dma, dma, dma]
        + [dma, dma, dma((3,)), dma((3,)), dma((3,)), dma((3,))]
        + [dma((CHUNKS,)), dma((CHUNKS,)), hops, hops, hops, hops, dma((CHUNKS,)), dma, dma((CHUNKS,))]
        + [pltpu.VMEM((64, DEPTH, HALF), BF16)] * CHUNKS,
        compiler_params=pltpu.CompilerParams(
            collective_id=0, has_side_effects=True, vmem_limit_bytes=63 << 20
        ),
        name="muon",
    )(owned_matrix, rollout_matrix, gradient, momentum[0], master_weight[0])
    return (moment[None], update[None], weight[None], rollout[None])


def solution(mesh):
    everyone = P(("grp", "dev"), None, None)
    return jax.shard_map(
        shards,
        mesh=mesh,
        in_specs=(P("grp", "dev", None), everyone, everyone, P(), P("grp", None)),
        out_specs=(everyone,) * 4,
        check_vma=False,
    )
```

```python
import math

import jax
import jax.numpy as jnp
from jax import lax
from jax.experimental import pallas as pl
from jax.experimental.pallas import tpu as pltpu
from jax.sharding import PartitionSpec as P

MESH = pl.DeviceIdType.MESH
F32 = jnp.float32
BF16 = jnp.bfloat16

ITERS = 5
momentum_decay = 0.95
learn_rate = 0.02
weight_decay = 0.1
first_coeff = 3.4445
second_coeff = -4.775
third_coeff = 2.0315
norm_epsilon = 1e-07

N = 512
HALF = 256
QUADS = 16
DEVS = 64
CHUNKS = 8
DEPTH = 16
TILES = [(i, j) for i in range(4) for j in range(i, 4)]
PIECE = len(TILES) * 128 // 4


def split2(value):
    high = value.astype(BF16)
    return high, (value - high.astype(F32)).astype(BF16)


def split3(value):
    high = value.astype(BF16)
    rest = value - high.astype(F32)
    mid = rest.astype(BF16)
    return high, mid, (rest - mid.astype(F32)).astype(BF16)


def dot(left, right):
    return jnp.dot(left, right, preferred_element_type=F32)


def dot_t(left, right):
    return lax.dot_general(left, right, (((1,), (1,)), ((), ())), preferred_element_type=F32)


def terms(count):
    pairs = [(i, j) for i in range(count) for j in range(count) if i + j < count]
    return sorted(pairs, key=lambda pair: -sum(pair))


SCHEDULE = [
    1, 11, 31, 21, 41, 12, 2, 32, 51, 13, 22, 3, 42, 14, 33, 61, 4, 23, 10, 34,
    52, 71, 0, 43, 24, 30, 62, 53, 44, 72, 20, 63, 54, 40, 73, 64, 50, 74, 60, 70,
]


def blocks_of(unit):
    return unit // 5, slice(unit % 5 * 64, (unit % 5 + 1) * 64)


def kernel(
    owned, wanted, grad_in, mom_in, master_in,
    mom_out, update_out, master_out, rollout_out,
    grad, mom, master, update,
    outbox, inbox, partial, others, full,
    a_ref, t_ref, x_ref,
    a0, a1, a2, b0, b1, b2, t0, t1, t2, x0, x1, x2, x3,
    rounded, chosen, names, table_v, table,
    in_sem, out_sem, names_send, names_recv, table_sem,
    send_sem, recv_sem, rs_send, rs_recv, ag_send, ag_recv,
    s1_send, s1_recv, up_send, up_recv, down_send, down_recv, s3_send, s3_recv, own_sem,
    *held,
):
    grp, dev = lax.axis_index("grp"), lax.axis_index("dev")
    x, z_hi, y = lax.rem(dev, 4), lax.rem(lax.div(dev, 4), 4), lax.div(dev, 16)
    z_lo, core = lax.div(grp, 2), lax.rem(grp, 2)
    z = z_hi * 2 + z_lo
    mine = y * 2 + core
    slot = z * 8 + mine

    def device(x, y, z, core):
        return (lax.rem(z, 2) * 2 + core, (y * 4 + lax.div(z, 2)) * 4 + x)

    def in_plane(index):
        across, along_y = lax.rem(lax.div(index, 2), 4), lax.div(index, 8)
        return (z_lo * 2 + lax.rem(index, 2), (along_y * 4 + z_hi) * 4 + across)

    here = (y * 4 + x) * 2 + core
    above, below = device(x, y, lax.rem(z + 1, 8), core), device(x, y, lax.rem(z + 7, 8), core)
    twin = (z_lo * 2 + 1 - core, dev)

    def remote(src, dst, sends, recvs, to):
        return pltpu.make_async_remote_copy(
            src_ref=src, dst_ref=dst, send_sem=sends, recv_sem=recvs, device_id=to, device_id_type=MESH
        )

    loads = [
        pltpu.make_async_copy(src, dst, in_sem.at[index])
        for index, (src, dst) in enumerate(
            ((grad_in, grad), (mom_in, mom), (master_in, master))
        )
    ]
    for copy in loads:
        copy.start()

    barrier = pltpu.get_barrier_semaphore()

    def greet(to):
        pl.semaphore_signal(barrier, inc=1, device_id=to, device_id_type=MESH)

    def greet_group(step, carry):
        greet((grp, lax.rem(dev + step, DEVS)))
        return carry

    def greet_plane(step, carry):
        greet((z_lo * 2 + 1 - core, in_plane(2 * step)[1]))
        return carry

    lax.fori_loop(1, DEVS, greet_group, 0)
    lax.fori_loop(0, 16, greet_plane, 0)
    greet(above)
    greet(below)

    names[0] = jnp.zeros((8, 128), jnp.int32)
    names[0, 0:1, 0:DEVS] = wanted[...]
    loads[0].wait()

    def fill(q, carry):
        rows = grad[owned[grp, q]].astype(F32)
        for c in range(4):
            left = rows[:, c * N : c * N + HALF]
            right = rows[:, c * N + HALF : (c + 1) * N]
            outbox[q * 4 + c] = jnp.concatenate([left, right], axis=0).astype(BF16)
        return carry

    lax.fori_loop(0, QUADS, fill, 0)
    pl.semaphore_wait(barrier, DEVS - 1 + 18)

    def send(step, carry):
        to = lax.rem(dev + step, DEVS)
        remote(outbox.at[to], inbox.at[dev], send_sem, recv_sem, (grp, to)).start()
        return carry

    lax.fori_loop(1, DEVS, send, 0)
    tell = remote(names.at[0], names.at[1], names_send, names_recv, twin)
    tell.start()
    inbox[dev] = outbox[dev]

    tell.wait_recv()
    found = [jnp.zeros((8, 128), jnp.int32), jnp.zeros((8, 128), jnp.int32)]
    own_names, twin_names = names[0], names[1]
    for group in range(4):
        for quad in range(QUADS):
            identity = group * QUADS + owned[group, quad]
            at = ((quad % 4) * 2 + group // 2) * 8 + (quad // 4) * 2 + group % 2
            found[0] = jnp.where(own_names == identity, at, found[0])
            found[1] = jnp.where(twin_names == identity, at, found[1])
    table_v[core] = found[0]
    table_v[1 - core] = found[1]
    lookup = pltpu.make_async_copy(table_v, table, table_sem)
    lookup.start()

    loads[1].wait()
    rest = pl.ds(0, DEVS - 1)
    everything = remote(
        outbox.at[rest], inbox.at[rest], send_sem, recv_sem, (grp, lax.rem(dev + 1, DEVS))
    )
    everything.wait_recv()

    a_parts, b_parts, t_parts = (a0, a1, a2), (b0, b1, b2), (t0, t1, t2)
    x_parts = ((x0, x1), (x2, x3))
    for r in range(4):
        got = inbox[pl.ds(r * 16, 16)].astype(F32)
        slab = jnp.concatenate(
            [got[:, :8, :].reshape(128, HALF), got[:, 8:, :].reshape(128, HALF)], axis=1
        )
        rows = slice(r * 128, (r + 1) * 128)
        moment = momentum_decay * mom[rows, :] + slab
        mom[rows, :] = moment
        nesterov = slab + momentum_decay * moment
        x_ref[rows, :] = nesterov
        for part_ref, part in zip(b_parts, split3(nesterov)):
            part_ref[rows, :] = part
    stores = [pltpu.make_async_copy(mom, mom_out, out_sem.at[0])]
    stores[0].start()

    at = 0
    for i in range(4):
        total = None
        for a, b in terms(3):
            term = dot_t(b_parts[a][i * 128 : (i + 1) * 128, :], b_parts[b][i * 128 :, :])
            total = term if total is None else total + term
        for j in range(4 - i):
            for h in range(2):
                piece, rows = blocks_of(2 * at + h)
                partial[piece, rows, :] = total[h * 64 : (h + 1) * 64, j * 128 : (j + 1) * 128]
            at += 1

    def share(step, src, dst, sends, recvs):
        to = (grp, dev - x + lax.rem(x + step, 4))
        return remote(src, dst, sends.at[step - 1], recvs.at[step - 1], to)

    scatter = [
        share(step, partial.at[lax.rem(x + step, 4)], others.at[step - 1], rs_send, rs_recv)
        for step in (2, 1, 3)
    ]
    for copy in scatter:
        copy.start()
    for copy in scatter:
        copy.wait_recv()
    full[x] = (partial[x] + others[0]) + (others[1] + others[2])
    gather = [share(step, full.at[x], full.at[x], ag_send, ag_recv) for step in (2, 1, 3)]
    for copy in gather:
        copy.start()
    for copy in gather:
        copy.wait_recv()

    trace = None
    for at, (i, j) in enumerate(TILES):
        halves = [blocks_of(2 * at + h) for h in range(2)]
        tile = jnp.concatenate([full[piece, rows, :] for piece, rows in halves], axis=0)
        a_ref[i * 128 : (i + 1) * 128, j * 128 : (j + 1) * 128] = tile
        if i != j:
            a_ref[j * 128 : (j + 1) * 128, i * 128 : (i + 1) * 128] = tile.T
        else:
            row = lax.broadcasted_iota(jnp.int32, (128, 128), 0)
            col = lax.broadcasted_iota(jnp.int32, (128, 128), 1)
            diagonal = jnp.where(row == col, tile, 0.0)
            trace = diagonal if trace is None else trace + diagonal
    trace = jnp.sum(jnp.sum(trace, axis=0, keepdims=True), axis=1, keepdims=True)
    factor = 1.0 / (jnp.sqrt(trace) + norm_epsilon)
    everywhere, high = slice(0, N), slice(HALF, N)

    def emit(value, rows, cols, whole, parts):
        if whole is not None:
            whole[rows, cols] = value
        for part_ref, part in zip(parts, split2(value) if len(parts) == 2 else split3(value)):
            part_ref[rows, cols] = part

    for r in range(4):
        rows = slice(r * 128, (r + 1) * 128)
        emit(x_ref[rows, :] * factor, rows, everywhere, x_ref, x_parts[0])
        emit(a_ref[rows, :] * (factor * factor), rows, everywhere, a_ref, a_parts)

    def block(lefts, rights, rows, cols, count):
        total = None
        for a, b in terms(count):
            term = dot(lefts[a][rows, :], rights[b][:, cols])
            total = term if total is None else total + term
        return total

    def symmetric(lefts, rights, count, finish, whole, parts):
        for r in range(4):
            rows = slice(r * 128, (r + 1) * 128)
            cols = everywhere if r < 2 else high
            value = finish(block(lefts, rights, rows, cols, count), rows, cols)
            emit(value, rows, cols, whole, parts)
            if r < 2:
                for s in range(2, 4):
                    mirror = slice(s * 128, (s + 1) * 128)
                    emit(value[:, mirror].T, mirror, rows, whole, parts)

    def iterate(step, count, following):
        symmetric(
            a_parts, a_parts, count,
            lambda v, r, c: second_coeff * a_ref[r, c] + third_coeff * v,
            None, b_parts[:count],
        )
        symmetric(
            b_parts, a_parts, count,
            lambda v, r, c: first_coeff * a_ref[r, c] + v,
            t_ref, t_parts[:count],
        )
        symmetric(
            b_parts, t_parts, count,
            lambda v, r, c: first_coeff * t_ref[r, c] + v,
            a_ref, a_parts[:following],
        )
        for r in range(4):
            rows = slice(r * 128, (r + 1) * 128)
            value = block(b_parts, x_parts[step % 2], rows, everywhere, 2)
            value = first_coeff * x_ref[rows, :] + value
            emit(value, rows, everywhere, x_ref, x_parts[(step + 1) % 2])

    for step, counts in enumerate(((3, 3), (3, 2), (2, 2), (2, 2))):
        iterate(step, *counts)

    def region(chunk, part):
        first = chunk // 2 * 128 + part * DEPTH
        return pl.ds(pl.multiple_of(first, DEPTH), DEPTH), slice(chunk % 2 * HALF, (chunk % 2 + 1) * HALF)

    def spread(chunk):
        part = held[chunk].at[pl.ds(0, 7)]
        return remote(part, part, s1_send.at[chunk], s1_recv.at[chunk], above)

    loads[2].wait()
    for r in range(4):
        rows = slice(r * 128, (r + 1) * 128)
        value = block(a_parts, a_parts, rows, everywhere, 2)
        emit(second_coeff * a_ref[rows, :] + third_coeff * value, rows, everywhere, None, b_parts[:2])
        value = block(b_parts, x_parts[0], rows, everywhere, 2)
        step = (first_coeff * x_ref[rows, :] + value) * (0.2 * math.sqrt(max(N, 4 * N)))
        update[rows, :] = step
        weight = master[rows, :]
        weight = weight - learn_rate * (step + weight_decay * weight)
        master[rows, :] = weight
        rounded[rows, :] = weight.astype(BF16)
        for chunk in (2 * r, 2 * r + 1):
            for away in range(1, 8):
                to = lax.rem(mine + away, 8)
                remote(
                    rounded.at[region(chunk, to)], held[chunk].at[slot],
                    s1_send.at[chunk], s1_recv.at[chunk],
                    device(x, lax.div(to, 2), z, lax.rem(to, 2)),
                ).start()
            held[chunk][slot] = rounded[region(chunk, mine)]
    stores += [
        pltpu.make_async_copy(update, update_out, out_sem.at[1]),
        pltpu.make_async_copy(master, master_out, out_sem.at[2]),
    ]
    stores[1].start()
    stores[2].start()
    lookup.wait()

    def along(chunk, step, up):
        count = 8 if step < 4 else 4
        plane = lax.rem(z + 9 - step, 8) if up else lax.rem(z + step - 1, 8)
        first = plane * 8 + (0 if up or step < 4 else 4)
        part = held[chunk].at[pl.ds(first, count)]
        index = chunk * 4 + step - 1
        if up:
            return remote(part, part, up_send.at[index], up_recv.at[index], above)
        return remote(part, part, down_send.at[index], down_recv.at[index], below)

    def goal(chunk):
        first = x * N + chunk % 2 * HALF
        return rollout_out.at[region(chunk, mine)[0], pl.ds(pl.multiple_of(first, HALF), HALF)]

    def pick(chunk, index):
        chosen[chunk, index] = held[chunk][table[lax.rem(index, 2), 0, in_plane(index)[1]]]

    def deliver(chunk):
        target = goal(chunk)

        def give(step, carry):
            index = lax.rem(here + step, 32)
            pick(chunk, index)
            remote(
                chosen.at[chunk, index], target, s3_send.at[chunk], s3_recv, in_plane(index)
            ).start()
            return carry

        lax.fori_loop(1, 32, give, 0)
        pick(chunk, here)
        pltpu.make_async_copy(chosen.at[chunk, here], target, own_sem.at[chunk]).start()

    for code in SCHEDULE:
        chunk, step = code // 10, code % 10
        if step == 1:
            spread(chunk).wait_recv()
        else:
            hop = step - 1 if step else 4
            along(chunk, hop, True).wait_recv()
            along(chunk, hop, False).wait_recv()
        if step:
            along(chunk, step, True).start()
            along(chunk, step, False).start()
        else:
            deliver(chunk)

    tell.wait_send()
    everything.wait_send()
    for copy in scatter + gather:
        copy.wait_send()
    for copy in stores:
        copy.wait()
    for chunk in range(CHUNKS):
        spread(chunk).wait_send()
        for step in range(1, 5):
            along(chunk, step, True).wait_send()
            along(chunk, step, False).wait_send()
        part = chosen.at[chunk, pl.ds(0, 31)]
        remote(part, part, s3_send.at[chunk], s3_recv, above).wait_send()
        pltpu.make_async_copy(chosen.at[chunk, here], goal(chunk), own_sem.at[chunk]).wait()
    arrived = rollout_out.at[pl.ds(0, 31 * 16), :]
    remote(arrived, arrived, s3_send.at[0], s3_recv, above).wait_recv()


def publish_kernel(moment, update, weight, rollout, *refs):
    outs, (buffer, load_sem, store_sem) = refs[:4], refs[4:]
    loads, stores = [], []
    for index in range(4):
        rows = pl.ds(index * 128, 128)
        loads.append(
            pltpu.make_async_copy(rollout.at[rows, :], buffer.at[rows, :], load_sem.at[index])
        )
        loads[-1].start()
    for index, (src, dst) in enumerate(zip((moment, update, weight), outs)):
        stores.append(pltpu.make_async_copy(src, dst, store_sem.at[index]))
        stores[-1].start()
    for index in range(4):
        rows = pl.ds(index * 128, 128)
        loads[index].wait()
        stores.append(
            pltpu.make_async_copy(buffer.at[rows, :], outs[3].at[rows, :], store_sem.at[3 + index])
        )
        stores[-1].start()
    for copy in stores:
        copy.wait()


def publish_call(moment, update, weight, rollout):
    vmem, anywhere = pl.BlockSpec(memory_space=pltpu.VMEM), pl.BlockSpec(memory_space=pl.ANY)
    dma = pltpu.SemaphoreType.DMA
    results = (moment, update, weight, rollout)
    return pl.pallas_call(
        publish_kernel,
        out_shape=tuple(jax.ShapeDtypeStruct(v.shape, v.dtype) for v in results),
        in_specs=[vmem, vmem, vmem, anywhere],
        out_specs=(anywhere,) * 4,
        scratch_shapes=[pltpu.VMEM((N, 4 * N), BF16), dma((4,)), dma((7,))],
        compiler_params=pltpu.CompilerParams(vmem_limit_bytes=50 << 20),
        name="publish",
    )(*results)


def shards(gradient, momentum, master_weight, owned_matrix, rollout_matrix):
    smem, vmem, anywhere = (
        pl.BlockSpec(memory_space=space) for space in (pltpu.SMEM, pltpu.VMEM, pl.ANY)
    )
    dma = pltpu.SemaphoreType.DMA
    square = jax.ShapeDtypeStruct((N, N), F32)
    wide, half = pltpu.VMEM((N, N), F32), pltpu.VMEM((N, N), BF16)
    hops = dma((CHUNKS * 4,))
    box = pltpu.VMEM((DEVS, 16, HALF), BF16)
    moment, update, weight, rollout = pl.pallas_call(
        kernel,
        out_shape=(square, square, square, jax.ShapeDtypeStruct((N, 4 * N), BF16)),
        in_specs=[smem, vmem, anywhere, anywhere, anywhere],
        out_specs=(anywhere,) * 4,
        scratch_shapes=[pltpu.VMEM((QUADS, 8, 4 * N), BF16), wide, wide, wide]
        + [box, box]
        + [pltpu.VMEM((count, PIECE, 128), F32) for count in (4, 3, 4)]
        + [wide] * 3
        + [half] * 13
        + [
            half,
            pltpu.VMEM((CHUNKS, 32, DEPTH, HALF), BF16),
            pltpu.VMEM((2, 8, 128), jnp.int32),
            pltpu.VMEM((2, 8, 128), jnp.int32),
            pltpu.SMEM((2, 8, 128), jnp.int32),
        ]
        + [dma((3,)), dma((3,)), dma, dma, dma]
        + [dma, dma, dma((3,)), dma((3,)), dma((3,)), dma((3,))]
        + [dma((CHUNKS,)), dma((CHUNKS,)), hops, hops, hops, hops, dma((CHUNKS,)), dma, dma((CHUNKS,))]
        + [pltpu.VMEM((64, DEPTH, HALF), BF16)] * CHUNKS,
        compiler_params=pltpu.CompilerParams(
            collective_id=0, has_side_effects=True, vmem_limit_bytes=50 << 20
        ),
        name="muon",
    )(owned_matrix, rollout_matrix, gradient, momentum[0], master_weight[0])
    results = publish_call(moment, update, weight, rollout)
    return tuple(result[None] for result in results)


def solution(mesh):
    everyone = P(("grp", "dev"), None, None)
    return jax.shard_map(
        shards,
        mesh=mesh,
        in_specs=(P("grp", "dev", None), everyone, everyone, P(), P("grp", None)),
        out_specs=(everyone,) * 4,
        check_vma=False,
    )
```

```python
import math

import jax
import jax.numpy as jnp
from jax import lax
from jax.experimental import pallas as pl
from jax.experimental.pallas import tpu as pltpu
from jax.sharding import PartitionSpec as P

MESH = pl.DeviceIdType.MESH
F32 = jnp.float32
BF16 = jnp.bfloat16

ITERS = 5
momentum_decay = 0.95
learn_rate = 0.02
weight_decay = 0.1
first_coeff = 3.4445
second_coeff = -4.775
third_coeff = 2.0315
norm_epsilon = 1e-07

N = 512
HALF = 256
QUADS = 16
DEVS = 64
CHUNKS = 8
DEPTH = 16
TILES = [(i, j) for i in range(4) for j in range(i, 4)]


def split2(value):
    high = value.astype(BF16)
    return high, (value - high.astype(F32)).astype(BF16)


def split3(value):
    high = value.astype(BF16)
    rest = value - high.astype(F32)
    mid = rest.astype(BF16)
    return high, mid, (rest - mid.astype(F32)).astype(BF16)


def dot(left, right):
    return jnp.dot(left, right, preferred_element_type=F32)


def dot_t(left, right):
    return lax.dot_general(left, right, (((1,), (1,)), ((), ())), preferred_element_type=F32)


def terms(count):
    pairs = [(i, j) for i in range(count) for j in range(count) if i + j < count]
    return sorted(pairs, key=lambda pair: -sum(pair))


SCHEDULE = [
    1, 11, 31, 21, 41, 12, 2, 32, 51, 13, 22, 3, 42, 14, 33, 61, 4, 23, 10, 34,
    52, 71, 0, 43, 24, 30, 62, 53, 44, 72, 20, 63, 54, 40, 73, 64, 50, 74, 60, 70,
]


FIRST = 8
UNITS = (2, 3)


def blocks_of(unit):
    stage = 0 if unit < FIRST else 1
    unit = unit - FIRST * stage
    row = unit % UNITS[stage] * 64
    return stage, unit // UNITS[stage], slice(row, row + 64)


def kernel(
    owned, wanted, grad_in, mom_in, master_in,
    mom_out, update_out, master_out, rollout_out,
    grad, mom, master, update,
    outbox, inbox, partial_a, partial_b, others_a, others_b, full_a, full_b,
    a_ref, t_ref, x_ref,
    a0, a1, a2, b0, b1, b2, t0, t1, t2, x0, x1, x2, x3,
    rounded, chosen, names, table_v, table,
    in_sem, out_sem, names_send, names_recv, table_sem,
    send_sem, recv_sem, rs_send, rs_recv, ag_send, ag_recv,
    s1_send, s1_recv, up_send, up_recv, down_send, down_recv, s3_send, s3_recv, own_sem,
    *held,
):
    grp, dev = lax.axis_index("grp"), lax.axis_index("dev")
    x, z_hi, y = lax.rem(dev, 4), lax.rem(lax.div(dev, 4), 4), lax.div(dev, 16)
    z_lo, core = lax.div(grp, 2), lax.rem(grp, 2)
    z = z_hi * 2 + z_lo
    mine = y * 2 + core
    slot = z * 8 + mine

    def device(x, y, z, core):
        return (lax.rem(z, 2) * 2 + core, (y * 4 + lax.div(z, 2)) * 4 + x)

    def in_plane(index):
        across, along_y = lax.rem(lax.div(index, 2), 4), lax.div(index, 8)
        return (z_lo * 2 + lax.rem(index, 2), (along_y * 4 + z_hi) * 4 + across)

    here = (y * 4 + x) * 2 + core
    above, below = device(x, y, lax.rem(z + 1, 8), core), device(x, y, lax.rem(z + 7, 8), core)
    twin = (z_lo * 2 + 1 - core, dev)

    def remote(src, dst, sends, recvs, to):
        return pltpu.make_async_remote_copy(
            src_ref=src, dst_ref=dst, send_sem=sends, recv_sem=recvs, device_id=to, device_id_type=MESH
        )

    loads = [
        pltpu.make_async_copy(src, dst, in_sem.at[index])
        for index, (src, dst) in enumerate(
            ((grad_in, grad), (mom_in, mom), (master_in, master))
        )
    ]
    for copy in loads:
        copy.start()

    barrier = pltpu.get_barrier_semaphore()

    def greet(to):
        pl.semaphore_signal(barrier, inc=1, device_id=to, device_id_type=MESH)

    def greet_group(step, carry):
        greet((grp, lax.rem(dev + step, DEVS)))
        return carry

    def greet_plane(step, carry):
        greet((z_lo * 2 + 1 - core, in_plane(2 * step)[1]))
        return carry

    lax.fori_loop(1, DEVS, greet_group, 0)
    lax.fori_loop(0, 16, greet_plane, 0)
    greet(above)
    greet(below)

    names[0] = jnp.zeros((8, 128), jnp.int32)
    names[0, 0:1, 0:DEVS] = wanted[...]
    loads[0].wait()

    def fill(q, carry):
        rows = grad[owned[grp, q]].astype(F32)
        for c in range(4):
            left = rows[:, c * N : c * N + HALF]
            right = rows[:, c * N + HALF : (c + 1) * N]
            outbox[q * 4 + c] = jnp.concatenate([left, right], axis=0).astype(BF16)
        return carry

    lax.fori_loop(0, QUADS, fill, 0)
    pl.semaphore_wait(barrier, DEVS - 1 + 18)

    def send(step, carry):
        to = lax.rem(dev + step, DEVS)
        remote(outbox.at[to], inbox.at[dev], send_sem, recv_sem, (grp, to)).start()
        return carry

    lax.fori_loop(1, DEVS, send, 0)
    tell = remote(names.at[0], names.at[1], names_send, names_recv, twin)
    tell.start()
    inbox[dev] = outbox[dev]

    tell.wait_recv()
    found = [jnp.zeros((8, 128), jnp.int32), jnp.zeros((8, 128), jnp.int32)]
    own_names, twin_names = names[0], names[1]
    for group in range(4):
        for quad in range(QUADS):
            identity = group * QUADS + owned[group, quad]
            at = ((quad % 4) * 2 + group // 2) * 8 + (quad // 4) * 2 + group % 2
            found[0] = jnp.where(own_names == identity, at, found[0])
            found[1] = jnp.where(twin_names == identity, at, found[1])
    table_v[core] = found[0]
    table_v[1 - core] = found[1]
    lookup = pltpu.make_async_copy(table_v, table, table_sem)
    lookup.start()

    loads[1].wait()
    rest = pl.ds(0, DEVS - 1)
    everything = remote(
        outbox.at[rest], inbox.at[rest], send_sem, recv_sem, (grp, lax.rem(dev + 1, DEVS))
    )
    everything.wait_recv()

    a_parts, b_parts, t_parts = (a0, a1, a2), (b0, b1, b2), (t0, t1, t2)
    x_parts = ((x0, x1), (x2, x3))
    for r in range(4):
        got = inbox[pl.ds(r * 16, 16)].astype(F32)
        slab = jnp.concatenate(
            [got[:, :8, :].reshape(128, HALF), got[:, 8:, :].reshape(128, HALF)], axis=1
        )
        rows = slice(r * 128, (r + 1) * 128)
        moment = momentum_decay * mom[rows, :] + slab
        mom[rows, :] = moment
        nesterov = slab + momentum_decay * moment
        x_ref[rows, :] = nesterov
        for part_ref, part in zip(b_parts, split3(nesterov)):
            part_ref[rows, :] = part
    stores = [pltpu.make_async_copy(mom, mom_out, out_sem.at[0])]
    stores[0].start()

    partial, others, full = (partial_a, partial_b), (others_a, others_b), (full_a, full_b)

    def share(stage, step, src, dst, sends, recvs):
        to, index = (grp, dev - x + lax.rem(x + step, 4)), stage * 3 + step - 1
        return remote(src, dst, sends.at[index], recvs.at[index], to)

    scatter, gather = [], []

    def start_scatter(stage):
        for step in (2, 1, 3):
            src, dst = partial[stage].at[lax.rem(x + step, 4)], others[stage].at[step - 1]
            scatter.append(share(stage, step, src, dst, rs_send, rs_recv))
            scatter[-1].start()

    at = 0
    for i in range(4):
        total = None
        for a, b in terms(3):
            term = dot_t(b_parts[a][i * 128 : (i + 1) * 128, :], b_parts[b][i * 128 :, :])
            total = term if total is None else total + term
        for j in range(4 - i):
            for h in range(2):
                stage, piece, rows = blocks_of(2 * at + h)
                partial[stage][piece, rows, :] = total[
                    h * 64 : (h + 1) * 64, j * 128 : (j + 1) * 128
                ]
            at += 1
        if i == 0:
            start_scatter(0)
    start_scatter(1)
    for stage in range(2):
        for copy in scatter[stage * 3 : stage * 3 + 3]:
            copy.wait_recv()
        mine_part, theirs = partial[stage][x], others[stage]
        full[stage][x] = (mine_part + theirs[0]) + (theirs[1] + theirs[2])
        for step in (2, 1, 3):
            block_ref = full[stage].at[x]
            gather.append(share(stage, step, block_ref, block_ref, ag_send, ag_recv))
            gather[-1].start()
    for copy in gather:
        copy.wait_recv()

    trace = None
    for at, (i, j) in enumerate(TILES):
        halves = [blocks_of(2 * at + h) for h in range(2)]
        tile = jnp.concatenate(
            [full[stage][piece, rows, :] for stage, piece, rows in halves], axis=0
        )
        a_ref[i * 128 : (i + 1) * 128, j * 128 : (j + 1) * 128] = tile
        if i != j:
            a_ref[j * 128 : (j + 1) * 128, i * 128 : (i + 1) * 128] = tile.T
        else:
            row = lax.broadcasted_iota(jnp.int32, (128, 128), 0)
            col = lax.broadcasted_iota(jnp.int32, (128, 128), 1)
            diagonal = jnp.where(row == col, tile, 0.0)
            trace = diagonal if trace is None else trace + diagonal
    trace = jnp.sum(jnp.sum(trace, axis=0, keepdims=True), axis=1, keepdims=True)
    factor = 1.0 / (jnp.sqrt(trace) + norm_epsilon)
    everywhere, high = slice(0, N), slice(HALF, N)

    def emit(value, rows, cols, whole, parts):
        if whole is not None:
            whole[rows, cols] = value
        for part_ref, part in zip(parts, split2(value) if len(parts) == 2 else split3(value)):
            part_ref[rows, cols] = part

    for r in range(4):
        rows = slice(r * 128, (r + 1) * 128)
        emit(x_ref[rows, :] * factor, rows, everywhere, x_ref, x_parts[0])
        emit(a_ref[rows, :] * (factor * factor), rows, everywhere, a_ref, a_parts)

    def block(lefts, rights, rows, cols, count):
        total = None
        for a, b in terms(count):
            term = dot(lefts[a][rows, :], rights[b][:, cols])
            total = term if total is None else total + term
        return total

    def symmetric(lefts, rights, count, finish, whole, parts):
        for r in range(4):
            rows = slice(r * 128, (r + 1) * 128)
            cols = everywhere if r < 2 else high
            value = finish(block(lefts, rights, rows, cols, count), rows, cols)
            emit(value, rows, cols, whole, parts)
            if r < 2:
                for s in range(2, 4):
                    mirror = slice(s * 128, (s + 1) * 128)
                    emit(value[:, mirror].T, mirror, rows, whole, parts)

    def iterate(step, count, following):
        symmetric(
            a_parts, a_parts, count,
            lambda v, r, c: second_coeff * a_ref[r, c] + third_coeff * v,
            None, b_parts[:count],
        )
        symmetric(
            b_parts, a_parts, count,
            lambda v, r, c: first_coeff * a_ref[r, c] + v,
            t_ref, t_parts[:count],
        )
        symmetric(
            b_parts, t_parts, count,
            lambda v, r, c: first_coeff * t_ref[r, c] + v,
            a_ref, a_parts[:following],
        )
        for r in range(4):
            rows = slice(r * 128, (r + 1) * 128)
            value = block(b_parts, x_parts[step % 2], rows, everywhere, 2)
            value = first_coeff * x_ref[rows, :] + value
            emit(value, rows, everywhere, x_ref, x_parts[(step + 1) % 2])

    for step, counts in enumerate(((3, 3), (3, 2), (2, 2), (2, 2))):
        iterate(step, *counts)

    def region(chunk, part):
        first = chunk // 2 * 128 + part * DEPTH
        return pl.ds(pl.multiple_of(first, DEPTH), DEPTH), slice(chunk % 2 * HALF, (chunk % 2 + 1) * HALF)

    def spread(chunk):
        part = held[chunk].at[pl.ds(0, 7)]
        return remote(part, part, s1_send.at[chunk], s1_recv.at[chunk], above)

    loads[2].wait()
    for r in range(4):
        rows = slice(r * 128, (r + 1) * 128)
        value = block(a_parts, a_parts, rows, everywhere, 2)
        emit(second_coeff * a_ref[rows, :] + third_coeff * value, rows, everywhere, None, b_parts[:2])
        value = block(b_parts, x_parts[0], rows, everywhere, 2)
        step = (first_coeff * x_ref[rows, :] + value) * (0.2 * math.sqrt(max(N, 4 * N)))
        update[rows, :] = step
        weight = master[rows, :]
        weight = weight - learn_rate * (step + weight_decay * weight)
        master[rows, :] = weight
        rounded[rows, :] = weight.astype(BF16)
        for chunk in (2 * r, 2 * r + 1):
            for away in range(1, 8):
                to = lax.rem(mine + away, 8)
                remote(
                    rounded.at[region(chunk, to)], held[chunk].at[slot],
                    s1_send.at[chunk], s1_recv.at[chunk],
                    device(x, lax.div(to, 2), z, lax.rem(to, 2)),
                ).start()
            held[chunk][slot] = rounded[region(chunk, mine)]
    stores += [
        pltpu.make_async_copy(update, update_out, out_sem.at[1]),
        pltpu.make_async_copy(master, master_out, out_sem.at[2]),
    ]
    stores[1].start()
    stores[2].start()
    lookup.wait()

    def along(chunk, step, up):
        count = 8 if step < 4 else 4
        plane = lax.rem(z + 9 - step, 8) if up else lax.rem(z + step - 1, 8)
        first = plane * 8 + (0 if up or step < 4 else 4)
        part = held[chunk].at[pl.ds(first, count)]
        index = chunk * 4 + step - 1
        if up:
            return remote(part, part, up_send.at[index], up_recv.at[index], above)
        return remote(part, part, down_send.at[index], down_recv.at[index], below)

    def goal(chunk):
        first = x * N + chunk % 2 * HALF
        return rollout_out.at[region(chunk, mine)[0], pl.ds(pl.multiple_of(first, HALF), HALF)]

    def pick(chunk, index):
        chosen[chunk, index] = held[chunk][table[lax.rem(index, 2), 0, in_plane(index)[1]]]

    def deliver(chunk):
        target = goal(chunk)

        def give(step, carry):
            index = lax.rem(here + step, 32)
            pick(chunk, index)
            remote(
                chosen.at[chunk, index], target, s3_send.at[chunk], s3_recv, in_plane(index)
            ).start()
            return carry

        lax.fori_loop(1, 32, give, 0)
        pick(chunk, here)
        pltpu.make_async_copy(chosen.at[chunk, here], target, own_sem.at[chunk]).start()

    for code in SCHEDULE:
        chunk, step = code // 10, code % 10
        if step == 1:
            spread(chunk).wait_recv()
        else:
            hop = step - 1 if step else 4
            along(chunk, hop, True).wait_recv()
            along(chunk, hop, False).wait_recv()
        if step:
            along(chunk, step, True).start()
            along(chunk, step, False).start()
        else:
            deliver(chunk)

    tell.wait_send()
    everything.wait_send()
    for copy in scatter + gather:
        copy.wait_send()
    for copy in stores:
        copy.wait()
    for chunk in range(CHUNKS):
        spread(chunk).wait_send()
        for step in range(1, 5):
            along(chunk, step, True).wait_send()
            along(chunk, step, False).wait_send()
        part = chosen.at[chunk, pl.ds(0, 31)]
        remote(part, part, s3_send.at[chunk], s3_recv, above).wait_send()
        pltpu.make_async_copy(chosen.at[chunk, here], goal(chunk), own_sem.at[chunk]).wait()
    arrived = rollout_out.at[pl.ds(0, 31 * 16), :]
    remote(arrived, arrived, s3_send.at[0], s3_recv, above).wait_recv()


def publish_kernel(*refs):
    sources, targets, buffers, (load_sem, store_sem) = refs[:4], refs[4:8], refs[8:12], refs[12:]
    loads = [
        pltpu.make_async_copy(sources[index], buffers[index], load_sem.at[index])
        for index in range(4)
    ]
    stores = [
        pltpu.make_async_copy(buffers[index], targets[index], store_sem.at[index])
        for index in range(4)
    ]
    for copy in loads:
        copy.start()
    for load, store in zip(loads, stores):
        load.wait()
        store.start()
    for copy in stores:
        copy.wait()


def publish_call(*results):
    anywhere, dma = pl.BlockSpec(memory_space=pl.ANY), pltpu.SemaphoreType.DMA
    return pl.pallas_call(
        publish_kernel,
        out_shape=tuple(jax.ShapeDtypeStruct(v.shape, v.dtype) for v in results),
        in_specs=[anywhere] * 4,
        out_specs=(anywhere,) * 4,
        scratch_shapes=[pltpu.VMEM(v.shape, v.dtype) for v in results] + [dma((4,)), dma((4,))],
        compiler_params=pltpu.CompilerParams(vmem_limit_bytes=63 << 20),
        name="publish",
    )(*results)


def shards(gradient, momentum, master_weight, owned_matrix, rollout_matrix):
    smem, vmem, anywhere = (
        pl.BlockSpec(memory_space=space) for space in (pltpu.SMEM, pltpu.VMEM, pl.ANY)
    )
    dma = pltpu.SemaphoreType.DMA
    square = jax.ShapeDtypeStruct((N, N), F32)
    wide, half = pltpu.VMEM((N, N), F32), pltpu.VMEM((N, N), BF16)
    hops = dma((CHUNKS * 4,))
    box = pltpu.VMEM((DEVS, 16, HALF), BF16)
    moment, update, weight, rollout = pl.pallas_call(
        kernel,
        out_shape=(square, square, square, jax.ShapeDtypeStruct((N, 4 * N), BF16)),
        in_specs=[smem, vmem, anywhere, anywhere, anywhere],
        out_specs=(anywhere,) * 4,
        scratch_shapes=[pltpu.VMEM((QUADS, 8, 4 * N), BF16), wide, wide, wide]
        + [box, box]
        + [pltpu.VMEM((count, units * 64, 128), F32) for count in (4, 3, 4) for units in UNITS]
        + [wide] * 3
        + [half] * 13
        + [
            half,
            pltpu.VMEM((CHUNKS, 32, DEPTH, HALF), BF16),
            pltpu.VMEM((2, 8, 128), jnp.int32),
            pltpu.VMEM((2, 8, 128), jnp.int32),
            pltpu.SMEM((2, 8, 128), jnp.int32),
        ]
        + [dma((3,)), dma((3,)), dma, dma, dma]
        + [dma, dma, dma((6,)), dma((6,)), dma((6,)), dma((6,))]
        + [dma((CHUNKS,)), dma((CHUNKS,)), hops, hops, hops, hops, dma((CHUNKS,)), dma, dma((CHUNKS,))]
        + [pltpu.VMEM((64, DEPTH, HALF), BF16)] * CHUNKS,
        compiler_params=pltpu.CompilerParams(
            collective_id=0, has_side_effects=True, vmem_limit_bytes=63 << 20
        ),
        name="muon",
    )(owned_matrix, rollout_matrix, gradient, momentum[0], master_weight[0])
    results = publish_call(moment, update, weight, rollout)
    return tuple(result[None] for result in results)


def solution(mesh):
    everyone = P(("grp", "dev"), None, None)
    return jax.shard_map(
        shards,
        mesh=mesh,
        in_specs=(P("grp", "dev", None), everyone, everyone, P(), P("grp", None)),
        out_specs=(everyone,) * 4,
        check_vma=False,
    )
```

```python
import math

import jax
import jax.numpy as jnp
from jax import lax
from jax.experimental import pallas as pl
from jax.experimental.pallas import tpu as pltpu
from jax.sharding import PartitionSpec as P

MESH = pl.DeviceIdType.MESH
F32 = jnp.float32
BF16 = jnp.bfloat16

ITERS = 5
momentum_decay = 0.95
learn_rate = 0.02
weight_decay = 0.1
first_coeff = 3.4445
second_coeff = -4.775
third_coeff = 2.0315
norm_epsilon = 1e-07

N = 512
HALF = 256
QUADS = 16
DEVS = 64
CHUNKS = 8
DEPTH = 16
TILES = [(i, j) for i in range(4) for j in range(i, 4)]


def split2(value):
    high = value.astype(BF16)
    return high, (value - high.astype(F32)).astype(BF16)


def split3(value):
    high = value.astype(BF16)
    rest = value - high.astype(F32)
    mid = rest.astype(BF16)
    return high, mid, (rest - mid.astype(F32)).astype(BF16)


def dot(left, right):
    return jnp.dot(left, right, preferred_element_type=F32)


def dot_t(left, right):
    return lax.dot_general(left, right, (((1,), (1,)), ((), ())), preferred_element_type=F32)


def terms(count):
    pairs = [(i, j) for i in range(count) for j in range(count) if i + j < count]
    return sorted(pairs, key=lambda pair: -sum(pair))


SCHEDULE = [
    1, 11, 31, 21, 41, 12, 2, 32, 51, 13, 22, 3, 42, 14, 33, 61, 4, 23, 10, 34,
    52, 71, 0, 43, 24, 30, 62, 53, 44, 72, 20, 63, 54, 40, 73, 64, 50, 74, 60, 70,
]


FIRST = 8
UNITS = (2, 3)


def blocks_of(unit):
    stage = 0 if unit < FIRST else 1
    unit = unit - FIRST * stage
    row = unit % UNITS[stage] * 64
    return stage, unit // UNITS[stage], slice(row, row + 64)


def kernel(
    owned, wanted, grad_in, mom_in, master_in,
    mom_out, update_out, master_out, rollout_out,
    grad, mom, master, update,
    outbox, inbox, partial_a, partial_b, others_a, others_b, full_a, full_b,
    a_ref, t_ref, x_ref,
    a0, a1, a2, b0, b1, b2, t0, t1, t2, x0, x1, x2, x3,
    rounded, chosen, names, table_v, table,
    in_sem, out_sem, names_send, names_recv, table_sem,
    send_sem, recv_sem, rs_send, rs_recv, ag_send, ag_recv,
    s1_send, s1_recv, up_send, up_recv, down_send, down_recv, s3_send, s3_recv, own_sem,
    *held,
):
    grp, dev = lax.axis_index("grp"), lax.axis_index("dev")
    x, z_hi, y = lax.rem(dev, 4), lax.rem(lax.div(dev, 4), 4), lax.div(dev, 16)
    z_lo, core = lax.div(grp, 2), lax.rem(grp, 2)
    z = z_hi * 2 + z_lo
    mine = y * 2 + core
    slot = z * 8 + mine

    def device(x, y, z, core):
        return (lax.rem(z, 2) * 2 + core, (y * 4 + lax.div(z, 2)) * 4 + x)

    def in_plane(index):
        across, along_y = lax.rem(lax.div(index, 2), 4), lax.div(index, 8)
        return (z_lo * 2 + lax.rem(index, 2), (along_y * 4 + z_hi) * 4 + across)

    here = (y * 4 + x) * 2 + core
    above, below = device(x, y, lax.rem(z + 1, 8), core), device(x, y, lax.rem(z + 7, 8), core)
    twin = (z_lo * 2 + 1 - core, dev)

    def remote(src, dst, sends, recvs, to):
        return pltpu.make_async_remote_copy(
            src_ref=src, dst_ref=dst, send_sem=sends, recv_sem=recvs, device_id=to, device_id_type=MESH
        )

    loads = [
        pltpu.make_async_copy(src, dst, in_sem.at[index])
        for index, (src, dst) in enumerate(
            ((grad_in, grad), (mom_in, mom), (master_in, master))
        )
    ]
    for copy in loads:
        copy.start()

    barrier = pltpu.get_barrier_semaphore()

    def greet(to):
        pl.semaphore_signal(barrier, inc=1, device_id=to, device_id_type=MESH)

    def greet_group(step, carry):
        greet((grp, lax.rem(dev + step, DEVS)))
        return carry

    def greet_plane(step, carry):
        greet((z_lo * 2 + 1 - core, in_plane(2 * step)[1]))
        return carry

    lax.fori_loop(1, DEVS, greet_group, 0, unroll=9)
    lax.fori_loop(0, 16, greet_plane, 0, unroll=8)
    greet(above)
    greet(below)

    names[0] = jnp.zeros((8, 128), jnp.int32)
    names[0, 0:1, 0:DEVS] = wanted[...]
    loads[0].wait()

    def fill(q, carry):
        rows = grad[owned[grp, q]].astype(F32)
        for c in range(4):
            left = rows[:, c * N : c * N + HALF]
            right = rows[:, c * N + HALF : (c + 1) * N]
            outbox[q * 4 + c] = jnp.concatenate([left, right], axis=0).astype(BF16)
        return carry

    lax.fori_loop(0, QUADS, fill, 0, unroll=4)
    pl.semaphore_wait(barrier, DEVS - 1 + 18)

    def send(step, carry):
        to = lax.rem(dev + step, DEVS)
        remote(outbox.at[to], inbox.at[dev], send_sem, recv_sem, (grp, to)).start()
        return carry

    lax.fori_loop(1, DEVS, send, 0, unroll=9)
    tell = remote(names.at[0], names.at[1], names_send, names_recv, twin)
    tell.start()
    inbox[dev] = outbox[dev]

    tell.wait_recv()
    found = [jnp.zeros((8, 128), jnp.int32), jnp.zeros((8, 128), jnp.int32)]
    own_names, twin_names = names[0], names[1]
    for group in range(4):
        for quad in range(QUADS):
            identity = group * QUADS + owned[group, quad]
            at = ((quad % 4) * 2 + group // 2) * 8 + (quad // 4) * 2 + group % 2
            found[0] = jnp.where(own_names == identity, at, found[0])
            found[1] = jnp.where(twin_names == identity, at, found[1])
    table_v[core] = found[0]
    table_v[1 - core] = found[1]
    lookup = pltpu.make_async_copy(table_v, table, table_sem)
    lookup.start()

    loads[1].wait()
    rest = pl.ds(0, DEVS - 1)
    everything = remote(
        outbox.at[rest], inbox.at[rest], send_sem, recv_sem, (grp, lax.rem(dev + 1, DEVS))
    )
    everything.wait_recv()

    a_parts, b_parts, t_parts = (a0, a1, a2), (b0, b1, b2), (t0, t1, t2)
    x_parts = ((x0, x1), (x2, x3))
    for r in range(4):
        got = inbox[pl.ds(r * 16, 16)].astype(F32)
        slab = jnp.concatenate(
            [got[:, :8, :].reshape(128, HALF), got[:, 8:, :].reshape(128, HALF)], axis=1
        )
        rows = slice(r * 128, (r + 1) * 128)
        moment = momentum_decay * mom[rows, :] + slab
        mom[rows, :] = moment
        nesterov = slab + momentum_decay * moment
        x_ref[rows, :] = nesterov
        for part_ref, part in zip(b_parts, split3(nesterov)):
            part_ref[rows, :] = part
    stores = [pltpu.make_async_copy(mom, mom_out, out_sem.at[0])]
    stores[0].start()

    partial, others, full = (partial_a, partial_b), (others_a, others_b), (full_a, full_b)

    def share(stage, step, src, dst, sends, recvs):
        to, index = (grp, dev - x + lax.rem(x + step, 4)), stage * 3 + step - 1
        return remote(src, dst, sends.at[index], recvs.at[index], to)

    scatter, gather = [], []

    def start_scatter(stage):
        for step in (2, 1, 3):
            src, dst = partial[stage].at[lax.rem(x + step, 4)], others[stage].at[step - 1]
            scatter.append(share(stage, step, src, dst, rs_send, rs_recv))
            scatter[-1].start()

    at = 0
    for i in range(4):
        total = None
        for a, b in terms(3):
            term = dot_t(b_parts[a][i * 128 : (i + 1) * 128, :], b_parts[b][i * 128 :, :])
            total = term if total is None else total + term
        for j in range(4 - i):
            for h in range(2):
                stage, piece, rows = blocks_of(2 * at + h)
                partial[stage][piece, rows, :] = total[
                    h * 64 : (h + 1) * 64, j * 128 : (j + 1) * 128
                ]
            at += 1
        if i == 0:
            start_scatter(0)
    start_scatter(1)
    for stage in range(2):
        for copy in scatter[stage * 3 : stage * 3 + 3]:
            copy.wait_recv()
        mine_part, theirs = partial[stage][x], others[stage]
        full[stage][x] = (mine_part + theirs[0]) + (theirs[1] + theirs[2])
        for step in (2, 1, 3):
            block_ref = full[stage].at[x]
            gather.append(share(stage, step, block_ref, block_ref, ag_send, ag_recv))
            gather[-1].start()
    for copy in gather:
        copy.wait_recv()

    trace = None
    for at, (i, j) in enumerate(TILES):
        halves = [blocks_of(2 * at + h) for h in range(2)]
        tile = jnp.concatenate(
            [full[stage][piece, rows, :] for stage, piece, rows in halves], axis=0
        )
        a_ref[i * 128 : (i + 1) * 128, j * 128 : (j + 1) * 128] = tile
        if i != j:
            a_ref[j * 128 : (j + 1) * 128, i * 128 : (i + 1) * 128] = tile.T
        else:
            row = lax.broadcasted_iota(jnp.int32, (128, 128), 0)
            col = lax.broadcasted_iota(jnp.int32, (128, 128), 1)
            diagonal = jnp.where(row == col, tile, 0.0)
            trace = diagonal if trace is None else trace + diagonal
    trace = jnp.sum(jnp.sum(trace, axis=0, keepdims=True), axis=1, keepdims=True)
    factor = 1.0 / (jnp.sqrt(trace) + norm_epsilon)
    everywhere, high = slice(0, N), slice(HALF, N)

    def emit(value, rows, cols, whole, parts):
        if whole is not None:
            whole[rows, cols] = value
        for part_ref, part in zip(parts, split2(value) if len(parts) == 2 else split3(value)):
            part_ref[rows, cols] = part

    for r in range(4):
        rows = slice(r * 128, (r + 1) * 128)
        emit(x_ref[rows, :] * factor, rows, everywhere, x_ref, x_parts[0])
        emit(a_ref[rows, :] * (factor * factor), rows, everywhere, a_ref, a_parts)

    def block(lefts, rights, rows, cols, count):
        total = None
        for a, b in terms(count):
            term = dot(lefts[a][rows, :], rights[b][:, cols])
            total = term if total is None else total + term
        return total

    def symmetric(lefts, rights, count, finish, whole, parts):
        for r in range(4):
            rows = slice(r * 128, (r + 1) * 128)
            cols = everywhere if r < 2 else high
            value = finish(block(lefts, rights, rows, cols, count), rows, cols)
            emit(value, rows, cols, whole, parts)
            if r < 2:
                for s in range(2, 4):
                    mirror = slice(s * 128, (s + 1) * 128)
                    emit(value[:, mirror].T, mirror, rows, whole, parts)

    def iterate(step, count, following):
        symmetric(
            a_parts, a_parts, count,
            lambda v, r, c: second_coeff * a_ref[r, c] + third_coeff * v,
            None, b_parts[:count],
        )
        symmetric(
            b_parts, a_parts, count,
            lambda v, r, c: first_coeff * a_ref[r, c] + v,
            t_ref, t_parts[:count],
        )
        symmetric(
            b_parts, t_parts, count,
            lambda v, r, c: first_coeff * t_ref[r, c] + v,
            a_ref, a_parts[:following],
        )
        for r in range(4):
            rows = slice(r * 128, (r + 1) * 128)
            value = block(b_parts, x_parts[step % 2], rows, everywhere, 2)
            value = first_coeff * x_ref[rows, :] + value
            emit(value, rows, everywhere, x_ref, x_parts[(step + 1) % 2])

    for step, counts in enumerate(((3, 3), (3, 2), (2, 2), (2, 2))):
        iterate(step, *counts)

    def region(chunk, part):
        first = chunk // 2 * 128 + part * DEPTH
        return pl.ds(pl.multiple_of(first, DEPTH), DEPTH), slice(chunk % 2 * HALF, (chunk % 2 + 1) * HALF)

    def spread(chunk):
        part = held[chunk].at[pl.ds(0, 7)]
        return remote(part, part, s1_send.at[chunk], s1_recv.at[chunk], above)

    loads[2].wait()
    for r in range(4):
        rows = slice(r * 128, (r + 1) * 128)
        value = block(a_parts, a_parts, rows, everywhere, 2)
        emit(second_coeff * a_ref[rows, :] + third_coeff * value, rows, everywhere, None, b_parts[:2])
        value = block(b_parts, x_parts[0], rows, everywhere, 2)
        step = (first_coeff * x_ref[rows, :] + value) * (0.2 * math.sqrt(max(N, 4 * N)))
        update[rows, :] = step
        weight = master[rows, :]
        weight = weight - learn_rate * (step + weight_decay * weight)
        master[rows, :] = weight
        rounded[rows, :] = weight.astype(BF16)
        for chunk in (2 * r, 2 * r + 1):
            for away in range(1, 8):
                to = lax.rem(mine + away, 8)
                remote(
                    rounded.at[region(chunk, to)], held[chunk].at[slot],
                    s1_send.at[chunk], s1_recv.at[chunk],
                    device(x, lax.div(to, 2), z, lax.rem(to, 2)),
                ).start()
            held[chunk][slot] = rounded[region(chunk, mine)]
    stores += [
        pltpu.make_async_copy(update, update_out, out_sem.at[1]),
        pltpu.make_async_copy(master, master_out, out_sem.at[2]),
    ]
    stores[1].start()
    stores[2].start()
    lookup.wait()

    def along(chunk, step, up):
        count = 8 if step < 4 else 4
        plane = lax.rem(z + 9 - step, 8) if up else lax.rem(z + step - 1, 8)
        first = plane * 8 + (0 if up or step < 4 else 4)
        part = held[chunk].at[pl.ds(first, count)]
        index = chunk * 4 + step - 1
        if up:
            return remote(part, part, up_send.at[index], up_recv.at[index], above)
        return remote(part, part, down_send.at[index], down_recv.at[index], below)

    def goal(chunk):
        first = x * N + chunk % 2 * HALF
        return rollout_out.at[region(chunk, mine)[0], pl.ds(pl.multiple_of(first, HALF), HALF)]

    def pick(chunk, index):
        chosen[chunk, index] = held[chunk][table[lax.rem(index, 2), 0, in_plane(index)[1]]]

    def deliver(chunk):
        target = goal(chunk)

        def give(step, carry):
            index = lax.rem(here + step, 32)
            pick(chunk, index)
            remote(
                chosen.at[chunk, index], target, s3_send.at[chunk], s3_recv, in_plane(index)
            ).start()
            return carry

        lax.fori_loop(1, 32, give, 0)
        pick(chunk, here)
        pltpu.make_async_copy(chosen.at[chunk, here], target, own_sem.at[chunk]).start()

    for code in SCHEDULE:
        chunk, step = code // 10, code % 10
        if step == 1:
            spread(chunk).wait_recv()
        else:
            hop = step - 1 if step else 4
            along(chunk, hop, True).wait_recv()
            along(chunk, hop, False).wait_recv()
        if step:
            along(chunk, step, True).start()
            along(chunk, step, False).start()
        else:
            deliver(chunk)

    tell.wait_send()
    everything.wait_send()
    for copy in scatter + gather:
        copy.wait_send()
    for copy in stores:
        copy.wait()
    for chunk in range(CHUNKS):
        spread(chunk).wait_send()
        for step in range(1, 5):
            along(chunk, step, True).wait_send()
            along(chunk, step, False).wait_send()
        part = chosen.at[chunk, pl.ds(0, 31)]
        remote(part, part, s3_send.at[chunk], s3_recv, above).wait_send()
        pltpu.make_async_copy(chosen.at[chunk, here], goal(chunk), own_sem.at[chunk]).wait()
    arrived = rollout_out.at[pl.ds(0, 31 * 16), :]
    remote(arrived, arrived, s3_send.at[0], s3_recv, above).wait_recv()


def publish_kernel(*refs):
    sources, targets, buffers, (load_sem, store_sem) = refs[:4], refs[4:8], refs[8:12], refs[12:]
    loads = [
        pltpu.make_async_copy(sources[index], buffers[index], load_sem.at[index])
        for index in range(4)
    ]
    stores = [
        pltpu.make_async_copy(buffers[index], targets[index], store_sem.at[index])
        for index in range(4)
    ]
    for copy in loads:
        copy.start()
    for load, store in zip(loads, stores):
        load.wait()
        store.start()
    for copy in stores:
        copy.wait()


def publish_call(*results):
    anywhere, dma = pl.BlockSpec(memory_space=pl.ANY), pltpu.SemaphoreType.DMA
    return pl.pallas_call(
        publish_kernel,
        out_shape=tuple(jax.ShapeDtypeStruct(v.shape, v.dtype) for v in results),
        in_specs=[anywhere] * 4,
        out_specs=(anywhere,) * 4,
        scratch_shapes=[pltpu.VMEM(v.shape, v.dtype) for v in results] + [dma((4,)), dma((4,))],
        compiler_params=pltpu.CompilerParams(vmem_limit_bytes=63 << 20),
        name="publish",
    )(*results)


def shards(gradient, momentum, master_weight, owned_matrix, rollout_matrix):
    smem, vmem, anywhere = (
        pl.BlockSpec(memory_space=space) for space in (pltpu.SMEM, pltpu.VMEM, pl.ANY)
    )
    dma = pltpu.SemaphoreType.DMA
    square = jax.ShapeDtypeStruct((N, N), F32)
    wide, half = pltpu.VMEM((N, N), F32), pltpu.VMEM((N, N), BF16)
    hops = dma((CHUNKS * 4,))
    box = pltpu.VMEM((DEVS, 16, HALF), BF16)
    moment, update, weight, rollout = pl.pallas_call(
        kernel,
        out_shape=(square, square, square, jax.ShapeDtypeStruct((N, 4 * N), BF16)),
        in_specs=[smem, vmem, anywhere, anywhere, anywhere],
        out_specs=(anywhere,) * 4,
        scratch_shapes=[pltpu.VMEM((QUADS, 8, 4 * N), BF16), wide, wide, wide]
        + [box, box]
        + [pltpu.VMEM((count, units * 64, 128), F32) for count in (4, 3, 4) for units in UNITS]
        + [wide] * 3
        + [half] * 13
        + [
            half,
            pltpu.VMEM((CHUNKS, 32, DEPTH, HALF), BF16),
            pltpu.VMEM((2, 8, 128), jnp.int32),
            pltpu.VMEM((2, 8, 128), jnp.int32),
            pltpu.SMEM((2, 8, 128), jnp.int32),
        ]
        + [dma((3,)), dma((3,)), dma, dma, dma]
        + [dma, dma, dma((6,)), dma((6,)), dma((6,)), dma((6,))]
        + [dma((CHUNKS,)), dma((CHUNKS,)), hops, hops, hops, hops, dma((CHUNKS,)), dma, dma((CHUNKS,))]
        + [pltpu.VMEM((64, DEPTH, HALF), BF16)] * CHUNKS,
        compiler_params=pltpu.CompilerParams(
            collective_id=0, has_side_effects=True, vmem_limit_bytes=63 << 20
        ),
        name="muon",
    )(owned_matrix, rollout_matrix, gradient, momentum[0], master_weight[0])
    results = publish_call(moment, update, weight, rollout)
    return tuple(result[None] for result in results)


def solution(mesh):
    everyone = P(("grp", "dev"), None, None)
    return jax.shard_map(
        shards,
        mesh=mesh,
        in_specs=(P("grp", "dev", None), everyone, everyone, P(), P("grp", None)),
        out_specs=(everyone,) * 4,
        check_vma=False,
    )
```
